512 devices in a mesh: lib: 16 (over x, y_hi, core), dom: 32 (over y_lo, z).
Axes of the slice: x: 4, y: 8 (y_hi: 2, y_lo: 4; y = y_hi * 4 + y_lo), z: 8, core: 2. Of those that a mesh axis runs over, the one named last changes fastest.
Arguments:
- images: bfloat16 [12288, 2, 9216], P(('lib', 'dom')), may hold values from -6 to 6
- classes: int32 [12288], P(('lib', 'dom')), may hold values from 0 to 7
- precision: float32 [12288], P(('lib', 'dom')), may hold values from 0.01 to 0.1
- counts: int32 [512], P(('lib', 'dom')), may hold values from 12 to 24, as said below
- shifts: int32 [9, 2], replicated, may hold values from -3 to 3
- ctf_table: float32 [8, 9216], replicated, may hold values from -1 to 1
- projections: bfloat16 [32, 2, 9216], P('lib'), may hold values from -1.71 to 1.71
Outputs:
- accum: float32 [32, 2, 9216], P('lib', None, 'dom')
- log_norm: float32 [12288], P(('lib', 'dom'))
The draws below stay inside these ranges and needn't reach their ends.
Inputs may be any that keep to these rules, and one draw needn't show every extreme that they name: `counts`: each device has between 12 and 24 live slots, the first ones; some device has all 24 live.
All inputs are finite; a program needn't handle non-finite values.
Results may differ from the reference program's by a relative error of at most 0.0049.
Values may be sent and summed in bfloat16 or wider, within the bound.
A program may use at most 128 MiB of HBM per device.

```python
import math
import jax
import jax.numpy as jnp
from jax import lax

FREQ = 96
HALF = 9216
SHIFTS = 9
CLASSES = 8
CAP = 24
POSES = 32
PARTICLES = 12288
N_LIB = 16
N_DOM = 32


def shared_integers(key):
    particle_class = jax.random.randint(jax.random.fold_in(key, 101), (PARTICLES,), 0, CLASSES, dtype=jnp.int32)
    trials = jax.random.randint(jax.random.fold_in(key, 102), (SHIFTS * 2,), -3, 4, dtype=jnp.int32)
    places = jax.random.randint(jax.random.fold_in(key, 103), (2,), 0, SHIFTS * 2 - 1, dtype=jnp.int32)
    lower_place = places[0]
    upper_place = (lower_place + 1 + places[1]) % (SHIFTS * 2)
    positions = jnp.arange(SHIFTS * 2, dtype=jnp.int32)
    trials = jnp.where(positions == lower_place, -3, trials)
    trials = jnp.where(positions == upper_place, 3, trials).astype(jnp.int32).reshape(SHIFTS, 2)
    source = jax.random.randint(jax.random.fold_in(key, 104), (PARTICLES,), 0, POSES, dtype=jnp.int32)
    offset = jax.random.randint(jax.random.fold_in(key, 105), (PARTICLES,), 0, SHIFTS, dtype=jnp.int32)
    return (particle_class, trials, source, offset)


def shared_floats(key):
    ctf_values = jax.random.uniform(jax.random.fold_in(key, 106), (CLASSES, HALF), jnp.float32, -1.0, 1.0)
    phases = jax.random.uniform(jax.random.fold_in(key, 107), (POSES, HALF), jnp.float32, -math.pi, math.pi)
    gains = jax.random.uniform(jax.random.fold_in(key, 108), (POSES, HALF), jnp.float32, 1.13, 1.7)
    library = jnp.stack([gains * jnp.cos(phases), gains * jnp.sin(phases)], axis=1)
    return (ctf_values, library)


def draw_classes(key, part):
    return shared_integers(key)[0]


def draw_shifts(key, part):
    return shared_integers(key)[1]


def draw_ctf_table(key, part):
    return shared_floats(key)[0]


def draw_projections(key, part):
    return shared_floats(key)[1].astype(jnp.bfloat16)


def draw_images(key, part):
    particle_class, trials, source, offset = shared_integers(key)
    ctf_values, library = shared_floats(key)
    key = jax.random.fold_in(key, 23)
    noise_key, level_key = jax.random.split(key, 2)
    levels = jax.random.uniform(level_key, (PARTICLES,), jnp.float32, 0.025, 0.06)
    coefficient = jnp.arange(HALF, dtype=jnp.int32)
    freq_x = (coefficient % FREQ).astype(jnp.float32)
    freq_y = (coefficient // FREQ - FREQ // 2).astype(jnp.float32)
    step_x = trials[:, 0].astype(jnp.float32)[:, None]
    step_y = trials[:, 1].astype(jnp.float32)[:, None]
    angles = 2.0 * math.pi / (2.0 * FREQ) * (step_x * freq_x[None, :] + step_y * freq_y[None, :])
    cosine = jnp.cos(angles)
    sine_table = jnp.sin(angles)

    def one_block(block_index):
        start = block_index * CAP
        classes_here = lax.dynamic_slice_in_dim(particle_class, start, CAP)
        sources_here = lax.dynamic_slice_in_dim(source, start, CAP)
        offsets_here = lax.dynamic_slice_in_dim(offset, start, CAP)
        levels_here = lax.dynamic_slice_in_dim(levels, start, CAP)
        block_key = jax.random.fold_in(noise_key, block_index)
        gaussian = jnp.clip(jax.random.normal(jax.random.fold_in(block_key, 1), (CAP, 2, HALF), jnp.float32), -5.5, 5.5)
        ctf_rows = ctf_values[classes_here]
        chosen = library[sources_here]
        cos_rows = cosine[offsets_here]
        sin_rows = sine_table[offsets_here]
        real_signal = chosen[:, 0, :] * cos_rows - chosen[:, 1, :] * sin_rows
        imag_signal = chosen[:, 1, :] * cos_rows + chosen[:, 0, :] * sin_rows
        factor = levels_here[:, None] * ctf_rows
        signal = jnp.stack([factor * real_signal, factor * imag_signal], axis=1)
        return signal + gaussian
    blocks = lax.map(one_block, jnp.arange(N_LIB * N_DOM, dtype=jnp.int32))
    return blocks.reshape(PARTICLES, 2, HALF).astype(jnp.bfloat16)


def draw_counts(key, part):
    key = jax.random.fold_in(key, 11)
    first, second = jax.random.split(key)
    total = N_LIB * N_DOM
    drawn = jax.random.randint(first, (total,), CAP // 2, CAP + 1, dtype=jnp.int32)
    chosen = jax.random.randint(second, (), 0, total, dtype=jnp.int32)
    return jnp.where(jnp.arange(total, dtype=jnp.int32) == chosen, CAP, drawn).astype(jnp.int32)


def shard_levels(rng, extent, shards, smallest, top_value):
    gain = 1.0
    for position, blocks in shards:
        steps = jax.random.uniform(jax.random.fold_in(jax.random.fold_in(rng, 6), position), (blocks,), jnp.float32, smallest / len(shards), top_value / len(shards))
        gain = gain * jnp.repeat(jnp.exp(steps), extent[position] // blocks).reshape((-1,) + (1,) * (len(extent) - 1 - position))
    return gain


def setup_inputs(seed: int = 0) -> dict:
    splits = jax.random.split(jax.random.key(seed), 8)
    return {
        "images": draw_images(jax.random.fold_in(splits[7], 71), 0),
        "classes": draw_classes(jax.random.fold_in(splits[7], 71), 0),
        "precision": jnp.clip(jnp.exp(math.log(0.1) - 2.3025851 * jax.random.uniform(splits[2], (PARTICLES,), jnp.float32) ** shard_levels(splits[2], (PARTICLES,), ((0, 512),), -0.2, 0.2)), 0.01, 0.1),
        "counts": draw_counts(jax.random.fold_in(splits[7], 71), 0),
        "shifts": draw_shifts(jax.random.fold_in(splits[7], 71), 0),
        "ctf_table": draw_ctf_table(jax.random.fold_in(splits[7], 71), 0),
        "projections": draw_projections(jax.random.fold_in(splits[7], 71), 0),
    }


def phase_tables(shifts, half):
    index = jnp.arange(half, dtype=jnp.int32)
    freq_x = (index % FREQ).astype(jnp.float32)
    freq_y = (index // FREQ - FREQ // 2).astype(jnp.float32)
    step_x = shifts[:, 0].astype(jnp.float32)[:, None]
    step_y = shifts[:, 1].astype(jnp.float32)[:, None]
    angle = (2.0 * jnp.pi / (2.0 * FREQ)) * (step_x * freq_x[None, :] + step_y * freq_y[None, :])
    return jnp.cos(angle), jnp.sin(angle)


def reference(images, classes, precision, counts, shifts, ctf_table, projections):
    cosine, sine = phase_tables(shifts, HALF)
    flat_proj = projections.reshape(POSES, 2 * HALF)
    proj_f = projections.astype(jnp.float32)
    pose_power = proj_f[:, 0, :] ** 2 + proj_f[:, 1, :] ** 2
    power = jnp.dot(ctf_table * ctf_table, pose_power.T, precision=lax.Precision.HIGHEST)
    devices = N_LIB * N_DOM
    image_blocks = images.reshape(devices, CAP, 2, HALF)
    class_blocks = classes.reshape(devices, CAP)
    prec_blocks = precision.reshape(devices, CAP)

    def one_block(total, inputs):
        block, klass, prec, count = inputs
        onehot = (klass[:, None] == jnp.arange(CLASSES, dtype=jnp.int32)[None, :]).astype(jnp.float32)
        ctf_rows = jnp.dot(onehot, ctf_table, precision=lax.Precision.HIGHEST)
        real_part = block[:, 0, :].astype(jnp.float32) * ctf_rows
        imag_part = block[:, 1, :].astype(jnp.float32) * ctf_rows
        re_s = real_part[:, None, :] * cosine[None] + imag_part[:, None, :] * sine[None]
        im_s = imag_part[:, None, :] * cosine[None] - real_part[:, None, :] * sine[None]
        shifted = jnp.concatenate([re_s, im_s], axis=2).astype(jnp.bfloat16).reshape(CAP * SHIFTS, 2 * HALF)
        cross = jnp.dot(shifted, flat_proj.T, preferred_element_type=jnp.float32).reshape(CAP, SHIFTS, POSES)
        class_power = jnp.dot(onehot, power, precision=lax.Precision.HIGHEST)
        score = prec[:, None, None] * (cross - 0.5 * class_power[:, None, :])
        live = jnp.arange(CAP, dtype=jnp.int32) < count
        top = jnp.max(score, axis=(1, 2))
        log_norm = top + jnp.log(jnp.sum(jnp.exp(score - top[:, None, None]), axis=(1, 2)))
        weight = jnp.exp(score - log_norm[:, None, None]) * live[:, None, None].astype(jnp.float32)
        weight = weight.astype(jnp.bfloat16).reshape(CAP * SHIFTS, POSES)
        re_b = real_part[:, None, :] * cosine[None] - imag_part[:, None, :] * sine[None]
        im_b = imag_part[:, None, :] * cosine[None] + real_part[:, None, :] * sine[None]
        back = jnp.concatenate([re_b, im_b], axis=2).astype(jnp.bfloat16).reshape(CAP * SHIFTS, 2 * HALF)
        total = total + jnp.dot(weight.T, back, preferred_element_type=jnp.float32)
        return total, jnp.where(live, log_norm, jnp.zeros_like(log_norm))

    start = jnp.zeros((POSES, 2 * HALF), jnp.float32)
    total, norms = lax.scan(one_block, start, (image_blocks, class_blocks, prec_blocks, counts))
    return total.reshape(POSES, 2, HALF), norms.reshape(PARTICLES)
```

```python
import functools

import jax
import jax.numpy as jnp
import numpy as np
from jax import lax
from jax.experimental import pallas as pl
from jax.experimental.pallas import tpu as pltpu
from jax.sharding import PartitionSpec as P

FREQ = 96
SHIFTS = 9
HALF = 9216
CLASSES = 8
CAP = 24
POSES = 32
TILES = 72
RAW = 2 * TILES
WIDE = 2 * HALF
ROWS = 224
BLOCK = 2 * RAW + 16
STEP = 2.0 * np.pi / (2.0 * FREQ)
UNIT = 80
CHUNKS = ((0, 12), (12, 6))
MESH = pl.DeviceIdType.MESH
F32 = jnp.float32
BF16 = jnp.bfloat16


def place():
    lib = lax.axis_index("lib")
    dom = lax.axis_index("dom")
    return lib // 4, (lib // 2) % 2, dom // 8, dom % 8, lib % 2


def device(x, y, z, core):
    return ((x * 2 + y // 4) * 2 + core, (y % 4) * 8 + z)


def kernel(
    classes_ref, precision_ref, counts_ref, shifts_ref, img_hbm, ctf_hbm, proj_hbm,
    accum_ref, norm_ref,
    img, ctf, raw, crow, shifted, back, lib_in, lib_f, lib_b, own_f,
    acc, core_out, core_in, x_out, x_in, y_own, y_out, y_in, z_own, z_out, z_in,
    local_sem, send_sem, recv_sem,
):
    x, yh, yl, z, core = place()
    y = yh * 4 + yl
    me = (x * 2 + yh) * 2 + core
    right, left, across = (x + 1) % 4, (x + 3) % 4, (x + 2) % 4
    mate = 1 - core
    slots = iter(range(100))

    def slot_of(px, pyh, pcore):
        return (px * 2 + pyh) * 2 + pcore

    def remote(src, dst, target):
        k = next(slots)
        return pltpu.make_async_remote_copy(
            src_ref=src, dst_ref=dst, send_sem=send_sem.at[k], recv_sem=recv_sem.at[k],
            device_id=target, device_id_type=MESH,
        )

    img_copy = pltpu.make_async_copy(img_hbm, img, local_sem.at[0])
    ctf_copy = pltpu.make_async_copy(ctf_hbm, ctf, local_sem.at[1])
    own_copy = pltpu.make_async_copy(proj_hbm, lib_in.at[me, pl.ds(0, 2 * RAW)], local_sem.at[2])
    own_copy.start()
    ctf_copy.start()
    img_copy.start()
    partners = [device((x + d) % 4, y, z, core) for d in range(1, 4)]
    partners += [device(x, (y + d) % 8, z, core) for d in range(1, 8)]
    partners += [device(x, y, (z + d) % 8, core) for d in range(1, 8)]
    partners += [device(x, y, z, mate)]
    barrier = pltpu.get_barrier_semaphore()
    for partner in partners:
        pl.semaphore_signal(barrier, inc=1, device_id=partner, device_id_type=MESH)

    own_copy.wait()
    ctf_copy.wait()
    own_f[...] = lib_in[me, pl.ds(0, 2 * RAW), :].astype(F32)
    lane = lax.broadcasted_iota(jnp.int32, (8, 128), 1)
    tile = jnp.zeros((8, 128), F32)
    for p in range(2):
        re = own_f[pl.ds(p * RAW, TILES, stride=2), :]
        im = own_f[pl.ds(p * RAW + 1, TILES, stride=2), :]
        both = re * re + im * im
        total = jnp.zeros((8, 128), F32)
        for t in range(TILES):
            c = ctf[:, t * 128:(t + 1) * 128]
            total = total + (c * c) * both[t:t + 1, :]
        power = jnp.sum(total, axis=1, keepdims=True)
        hi = power.astype(BF16).astype(F32)
        mid = (power - hi).astype(BF16).astype(F32)
        low = power - hi - mid
        column = core * 16 + p * 8 + x * 2 + yh
        for k, part in enumerate((hi, mid, low)):
            tile = tile + jnp.where(lane == column + 32 * k, part, 0.0)
    lib_in[me, pl.ds(2 * RAW, 16), :] = jnp.concatenate([tile, jnp.zeros((8, 128), F32)], axis=0).astype(BF16)

    pl.semaphore_wait(barrier, len(partners))

    sent = []

    def block_to(slot, target, rows=None):
        view = lib_in.at[slot] if rows is None else lib_in.at[slot, pl.ds(*rows)]
        return remote(view, view, target)

    FIRST, SECOND = (0, 160), (160, BLOCK - 160)
    sides = (device(right, y, z, core), device(left, y, z, core))
    pair = device(x, y, z, mate)
    own_sends = [block_to(me, sides[0]), block_to(me, sides[1]), block_to(me, pair)]
    other = slot_of(x, 1 - yh, core)
    up, down = device(x, (y + 1) % 8, z, core), device(x, (y + 7) % 8, z, core)
    cross_down = block_to(me, down)
    cross_up = block_to(me, up)
    inner_up = block_to(other, up)
    inner_down = block_to(other, down)

    @pl.when(yl == 0)
    def _():
        cross_down.start()

    @pl.when(yl == 3)
    def _():
        cross_up.start()

    for copy in own_sends:
        copy.start()
    sent += own_sends

    def column_of(row):
        r = lax.broadcasted_iota(jnp.int32, (CAP, CAP), 0)
        c = lax.broadcasted_iota(jnp.int32, (CAP, CAP), 1)
        return jnp.sum(jnp.where(r == c, jnp.broadcast_to(row, (CAP, CAP)), 0.0), axis=1, keepdims=True)

    klass = column_of(classes_ref[...].astype(F32))
    prec = column_of(precision_ref[...])
    kinds = lax.broadcasted_iota(jnp.int32, (CAP, CLASSES), 1).astype(F32)
    onehot = (klass == kinds).astype(F32)
    pick = jnp.concatenate([onehot, onehot, onehot], axis=1).astype(BF16)
    for k in range(9):
        cols = slice(k * 1024, (k + 1) * 1024)
        c = ctf[:, cols]
        hi = c.astype(BF16).astype(F32)
        mid = (c - hi).astype(BF16).astype(F32)
        low = c - hi - mid
        parts = jnp.concatenate([hi, mid, low], axis=0).astype(BF16)
        crow[:, cols] = jnp.dot(pick, parts, preferred_element_type=F32)

    row16 = lax.broadcasted_iota(jnp.int32, (16, 128), 0)
    step_x = jnp.zeros((16, 128), F32)
    step_y = jnp.zeros((16, 128), F32)
    for s in range(SHIFTS):
        step_x = jnp.where(row16 == s, shifts_ref[s, 0].astype(F32), step_x)
        step_y = jnp.where(row16 == s, shifts_ref[s, 1].astype(F32), step_y)
    fine = []
    lanes = lax.broadcasted_iota(jnp.int32, (16, 128), 1)
    for u in range(3):
        j = lanes + u * 128
        dy = (j >= 96).astype(jnp.int32) + (j >= 192).astype(jnp.int32) + (j >= 288).astype(jnp.int32)
        kx = j - 96 * dy
        angle = STEP * (step_x * kx.astype(F32) + step_y * dy.astype(F32))
        fine.append((jnp.cos(angle), jnp.sin(angle)))
    start = STEP * (step_y * float(-(FREQ // 2)))
    turn = STEP * (step_y * 4.0)
    turn_c, turn_s = jnp.cos(turn), jnp.sin(turn)

    img_copy.wait()

    def widen(n, carry):
        rows = pl.ds(pl.multiple_of(n * RAW, 16), RAW)
        raw[rows, :] = img[rows, :].astype(F32)
        return carry

    lax.fori_loop(0, CAP, widen, 0)
    zeros8 = jnp.zeros((8, 128), F32)

    def shift_tiles(q, carry):
        base_c, base_s = carry
        for u in range(3):
            t = 3 * q + u
            fc, fs = fine[u]
            cosine = fc * base_c - fs * base_s
            sine = fs * base_c + fc * base_s
            c_tile = crow[:, pl.ds(pl.multiple_of(t * 128, 128), 128)]
            real, imag = [], []
            for g in range(3):
                c = c_tile[8 * g:8 * g + 8, :]
                real.append(raw[pl.ds(g * 8 * RAW + 2 * t, 8, stride=RAW), :] * c)
                imag.append(raw[pl.ds(g * 8 * RAW + 2 * t + 1, 8, stride=RAW), :] * c)
            re_s, im_s, re_b, im_b = [], [], [], []
            for s in range(SHIFTS):
                cs = jnp.broadcast_to(cosine[s:s + 1, :], (8, 128))
                sn = jnp.broadcast_to(sine[s:s + 1, :], (8, 128))
                for g in range(3):
                    ac, bs = real[g] * cs, imag[g] * sn
                    bc, as_ = imag[g] * cs, real[g] * sn
                    re_s.append(ac + bs)
                    im_s.append(bc - as_)
                    re_b.append(ac - bs)
                    im_b.append(bc + as_)
            for dst, parts in ((shifted, (re_s, im_s)), (back, (re_b, im_b))):
                for k, part in enumerate(parts):
                    cols = pl.ds(pl.multiple_of(t * 256 + k * 128, 128), 128)
                    dst[:, cols] = jnp.concatenate(part + [zeros8], axis=0).astype(BF16)
        return base_c * turn_c - base_s * turn_s, base_s * turn_c + base_c * turn_s

    phase = (jnp.cos(start), jnp.sin(start))
    phase = lax.fori_loop(0, 8, shift_tiles, phase)

    @pl.when(yl == 0)
    def _():
        cross_up.wait_recv()
        inner_up.start()

    @pl.when(yl == 3)
    def _():
        cross_down.wait_recv()
        inner_down.start()

    @pl.when(yl == 1)
    def _():
        inner_up.wait_recv()

    @pl.when(yl == 2)
    def _():
        inner_down.wait_recv()

    other_sends = [block_to(other, sides[0]), block_to(other, sides[1]), block_to(other, pair)]
    for copy in other_sends:
        copy.start()
    sent += other_sends
    phase = lax.fori_loop(8, 16, shift_tiles, phase)

    def hand_on(h, sends):
        from_left, from_right = slot_of(left, h, core), slot_of(right, h, core)
        copies = [block_to(from_left, sides[0], FIRST), block_to(from_left, pair)]
        sends[0].wait_recv()
        for copy in copies:
            copy.start()
        more = [block_to(from_right, sides[1], SECOND), block_to(from_right, pair)]
        sends[1].wait_recv()
        for copy in more:
            copy.start()
        return copies + more

    def finish(h, copies):
        copies[0].wait_recv()
        copies[2].wait_recv()
        copy = block_to(slot_of(across, h, core), pair)
        copy.start()
        return copy

    own_on = hand_on(yh, own_sends)
    sent += own_on
    phase = lax.fori_loop(16, 24, shift_tiles, phase)
    own_last = finish(yh, own_on)
    other_on = hand_on(1 - yh, other_sends)
    other_last = finish(1 - yh, other_on)
    sent += [own_last] + other_on + [other_last]
    for copy in (own_sends[2], other_sends[2], own_on[1], own_on[3], own_last, other_on[1], other_on[3], other_last):
        copy.wait_recv()

    def widen_lib(k, carry):
        lib_f[pl.ds(pl.multiple_of(k * 2 * RAW, 16), 2 * RAW), :] = lib_in[k, pl.ds(0, 2 * RAW), :].astype(F32)
        return carry

    lax.fori_loop(0, 16, widen_lib, 0)
    powers = jnp.zeros((8, 128), F32)
    for k in range(16):
        powers = powers + lib_in[k, pl.ds(2 * RAW, 16), :].astype(F32)[0:8, :]
    power = powers[:, 0:32] + powers[:, 32:64] + powers[:, 64:96]

    def gather_tiles(q, carry):
        for u in range(4):
            t = q * 4 + u
            halves = []
            for k in range(2):
                parts = [
                    lib_f[pl.ds(c * 2 * RAW + p * RAW + 2 * t + k, 8, stride=4 * RAW), :]
                    for c in range(2) for p in range(2)
                ]
                halves.append(jnp.concatenate(parts, axis=0))
            cols = pl.ds(pl.multiple_of(t * 256, 256), 256)
            lib_b[:, cols] = jnp.concatenate(halves, axis=1).astype(BF16)
        return carry

    lax.fori_loop(0, TILES // 4, gather_tiles, 0)

    def cross_part(q, total):
        cols = pl.ds(pl.multiple_of(q * 4608, 4608), 4608)
        return total + lax.dot_general(
            shifted[:, cols], lib_b[:, cols], (((1,), (1,)), ((), ())), preferred_element_type=F32
        )

    cross = lax.fori_loop(0, 4, cross_part, jnp.zeros((ROWS, POSES), F32))
    class_power = jnp.zeros((CAP, POSES), F32)
    for k in range(CLASSES):
        class_power = class_power + jnp.where(klass == float(k), power[k:k + 1, :], 0.0)
    scores = [prec * (cross[s * CAP:(s + 1) * CAP, :] - 0.5 * class_power) for s in range(SHIFTS)]
    top = scores[0]
    for s in range(1, SHIFTS):
        top = jnp.maximum(top, scores[s])
    top = jnp.max(top, axis=1, keepdims=True)
    mass = jnp.exp(scores[0] - top)
    for s in range(1, SHIFTS):
        mass = mass + jnp.exp(scores[s] - top)
    log_norm = top + jnp.log(jnp.sum(mass, axis=1, keepdims=True))
    live = lax.broadcasted_iota(jnp.int32, (CAP, 1), 0) < counts_ref[0]
    r24 = lax.broadcasted_iota(jnp.int32, (CAP, 128), 0)
    c24 = lax.broadcasted_iota(jnp.int32, (CAP, 128), 1)
    shown = jnp.where(live, log_norm, 0.0)
    norm_ref[...] = jnp.sum(jnp.where(r24 == c24, shown, 0.0), axis=0, keepdims=True)
    weights = [jnp.where(live, jnp.exp(score - log_norm), 0.0) for score in scores]
    weight = jnp.concatenate(weights + [jnp.zeros((8, POSES), F32)], axis=0).astype(BF16)
    unit = lax.broadcasted_iota(jnp.int32, (POSES, POSES), 0) == lax.broadcasted_iota(jnp.int32, (POSES, POSES), 1)
    weight_t = lax.dot_general(
        unit.astype(F32).astype(BF16), weight, (((1,), (1,)), ((), ())), preferred_element_type=F32
    ).astype(BF16)

    for c in range(2):
        for g in range(32):
            acc[pl.ds(c * 2560 + g * UNIT + 72, 8), :] = zeros8
    core_sends = []
    for first, count in CHUNKS:
        low, high = first * 4, 48 if first == 0 else UNIT

        def sum_quarter(quarter, carry):
            cols = pl.ds(pl.multiple_of((quarter * 18 + first) * 256, 256), count * 256)
            part = jnp.dot(weight_t, back[:, cols], preferred_element_type=F32)
            for c in range(2):
                for p in range(2):
                    r = c * 16 + p * 8
                    for k in range(2 * count):
                        row = c * 2560 + quarter * UNIT + (first * 2 + k) * 2 + p
                        acc[pl.ds(row, 8, stride=4 * UNIT), :] = part[r:r + 8, k * 128:(k + 1) * 128]
            for g in range(8):
                rows = pl.ds(pl.multiple_of(mate * 2560 + (g * 4 + quarter) * UNIT + low, 16), high - low)
                core_out[g, quarter, pl.ds(low, high - low), :] = acc[rows, :].astype(BF16)
            return carry

        lax.fori_loop(0, 4, sum_quarter, 0)
        rows = pl.ds(low, high - low)
        copy = remote(core_out.at[:, :, rows], core_in.at[:, :, rows], pair)
        copy.start()
        core_sends.append(copy)
    sent += core_sends

    x_sends = []
    for (first, count), core_copy in zip(CHUNKS, core_sends):
        low, high = first * 4, 48 if first == 0 else UNIT
        rows = pl.ds(low, high - low)
        core_copy.wait_recv()
        copies = []
        for d in (2, 1, 3):
            px = (x + d) % 4
            for h in range(2):
                for quarter in range(4):
                    at = pl.ds(pl.multiple_of(core * 2560 + ((px * 2 + h) * 4 + quarter) * UNIT + low, 16), high - low)
                    part = acc[at, :] + core_in[px * 2 + h, quarter, rows, :].astype(F32)
                    x_out[d - 1, h, quarter, rows, :] = part.astype(BF16)
            copy = remote(
                x_out.at[d - 1, :, :, rows], x_in.at[d - 1, :, :, rows], device(px, y, z, core)
            )
            copy.start()
            copies.append(copy)
        x_sends.append(copies)
        sent += copies

    y_sends = []
    for (first, count), copies in zip(CHUNKS, x_sends):
        low, high = first * 4, 48 if first == 0 else UNIT
        rows = pl.ds(low, high - low)
        for copy in copies:
            copy.wait_recv()
        for h in range(2):
            for quarter in range(4):
                at = pl.ds(pl.multiple_of(core * 2560 + ((x * 2 + h) * 4 + quarter) * UNIT + low, 16), high - low)
                part = acc[at, :] + core_in[x * 2 + h, quarter, rows, :].astype(F32)
                for d in range(3):
                    part = part + x_in[d, h, quarter, rows, :].astype(F32)
                y_own[h * 4 + quarter, rows, :] = part
                y_out[h * 4 + quarter, rows, :] = part.astype(BF16)
        copies = []
        for d in (4, 3, 5, 2, 6, 1, 7):
            py = (y + d) % 8
            copy = remote(y_out.at[py, rows], y_in.at[d - 1, rows], device(x, py, z, core))
            copy.start()
            copies.append(copy)
        y_sends.append(copies)
        sent += copies

    for (first, count), copies in zip(CHUNKS, y_sends):
        low, high = first * 4, 48 if first == 0 else UNIT
        rows = pl.ds(low, high - low)
        for copy in copies:
            copy.wait_recv()
        part = y_own[y, rows, :]
        for d in range(7):
            part = part + y_in[d, rows, :].astype(F32)
        z_own[rows, :] = part

    for k in range(8):
        first = 36 * (k // 4) + 8 * (k % 4)
        part = z_own[first:first + 16, :]
        y_own[k, pl.ds(0, 16), :] = part
        z_out[k] = part.astype(BF16)
    z_sends = []
    for d in (4, 3, 5, 2, 6, 1, 7):
        pz = (z + d) % 8
        copy = remote(z_out.at[pz], z_in.at[d - 1], device(x, y, pz, core))
        copy.start()
        z_sends.append(copy)
    sent += z_sends
    for copy in z_sends:
        copy.wait_recv()
    part = y_own[z, pl.ds(0, 16), :]
    for d in range(7):
        part = part + z_in[d].astype(F32)
    skip = (z % 4) * 32
    turned = pltpu.roll(part, (128 - skip) % 128, 1)
    keep = lax.broadcasted_iota(jnp.int32, (4, 128), 1) < 128 - skip
    for t in range(3):
        piece = turned[4 * t:4 * t + 4, :]
        if t < 2:
            piece = jnp.where(keep, piece, turned[4 * t + 4:4 * t + 8, :])
        width = 128 if t < 2 else 32
        for p in range(2):
            for c in range(2):
                accum_ref[p, c:c + 1, t * 128:t * 128 + width] = piece[c * 2 + p:c * 2 + p + 1, 0:width]

    for copy in sent:
        copy.wait_send()

    @pl.when(yl == 0)
    def _():
        cross_down.wait_send()
        inner_up.wait_send()

    @pl.when(yl == 3)
    def _():
        cross_up.wait_send()
        inner_down.wait_send()


def body(images, classes, precision, counts, shifts, ctf_table, projections):
    raw_img = images.reshape(CAP, 2, TILES, 128).transpose(0, 2, 1, 3).reshape(CAP * RAW, 128)
    raw_proj = projections.reshape(2, 2, TILES, 128).transpose(0, 2, 1, 3).reshape(2 * RAW, 128)
    vmem = pl.BlockSpec(memory_space=pltpu.VMEM)
    smem = pl.BlockSpec(memory_space=pltpu.SMEM)
    anywhere = pl.BlockSpec(memory_space=pl.ANY)
    accum, norm = pl.pallas_call(
        kernel,
        out_shape=(
            jax.ShapeDtypeStruct((2, 2, HALF // 32), F32),
            jax.ShapeDtypeStruct((1, 128), F32),
        ),
        in_specs=[vmem, vmem, smem, smem, anywhere, anywhere, anywhere],
        out_specs=(vmem, vmem),
        scratch_shapes=[
            pltpu.VMEM((CAP * RAW, 128), BF16),
            pltpu.VMEM((CLASSES, HALF), F32),
            pltpu.VMEM((CAP * RAW, 128), F32),
            pltpu.VMEM((CAP, HALF), F32),
            pltpu.VMEM((ROWS, WIDE), BF16),
            pltpu.VMEM((ROWS, WIDE), BF16),
            pltpu.VMEM((16, BLOCK, 128), BF16),
            pltpu.VMEM((32 * RAW, 128), F32),
            pltpu.VMEM((POSES, WIDE), BF16),
            pltpu.VMEM((2 * RAW, 128), F32),
            pltpu.VMEM((64 * UNIT, 128), F32),
            pltpu.VMEM((8, 4, UNIT, 128), BF16),
            pltpu.VMEM((8, 4, UNIT, 128), BF16),
            pltpu.VMEM((3, 2, 4, UNIT, 128), BF16),
            pltpu.VMEM((3, 2, 4, UNIT, 128), BF16),
            pltpu.VMEM((8, UNIT, 128), F32),
            pltpu.VMEM((8, UNIT, 128), BF16),
            pltpu.VMEM((7, UNIT, 128), BF16),
            pltpu.VMEM((UNIT, 128), F32),
            pltpu.VMEM((8, 16, 128), BF16),
            pltpu.VMEM((7, 16, 128), BF16),
            pltpu.SemaphoreType.DMA((3,)),
            pltpu.SemaphoreType.DMA((64,)),
            pltpu.SemaphoreType.DMA((64,)),
        ],
        compiler_params=pltpu.CompilerParams(
            collective_id=0, has_side_effects=True, vmem_limit_bytes=56 * 1024 * 1024
        ),
        name="expectation",
    )(classes.reshape(1, CAP), precision.reshape(1, CAP), counts, shifts, raw_img, ctf_table, raw_proj)
    return accum, norm.reshape(128)[:CAP]


def solution(mesh):
    placed = (
        P(("lib", "dom"), None, None),
        P(("lib", "dom")),
        P(("lib", "dom")),
        P(("lib", "dom")),
        P(),
        P(),
        P("lib", None, None),
    )
    return jax.shard_map(
        body,
        mesh=mesh,
        in_specs=placed,
        out_specs=(P("lib", None, "dom"), P(("lib", "dom"))),
        check_vma=False,
    )
```

```python
import functools

import jax
import jax.numpy as jnp
import numpy as np
from jax import lax
from jax.experimental import pallas as pl
from jax.experimental.pallas import tpu as pltpu
from jax.sharding import PartitionSpec as P

FREQ = 96
SHIFTS = 9
HALF = 9216
CLASSES = 8
CAP = 24
POSES = 32
TILES = 72
RAW = 2 * TILES
WIDE = 2 * HALF
PAIR = 2 * CAP
ROWS = SHIFTS * PAIR
HALF_TILES = TILES // 2
BLOCK = HALF_TILES * 4
LIB_CHUNKS = ((0, 20), (20, 16))
STEP = 2.0 * np.pi / (2.0 * FREQ)
UNIT = 80
CHUNKS = ((0, 4, 0, 32), (4, 5, 32, 80))
MESH = pl.DeviceIdType.MESH
F32 = jnp.float32
BF16 = jnp.bfloat16


def place():
    lib = lax.axis_index("lib")
    dom = lax.axis_index("dom")
    return lib // 4, (lib // 2) % 2, dom // 8, dom % 8, lib % 2


def device(x, y, z, core):
    return ((x * 2 + y // 4) * 2 + core, (y % 4) * 8 + z)


def kernel(
    classes_hbm, precision_hbm, counts_hbm, shifts_hbm, img_hbm, ctf_hbm, proj_hbm,
    accum_ref, norm_ref,
    classes_v, precision_v, counts_v, shifts_v, proj,
    img, ctf, raw, crow, shifted, back, meta, own_f, own_r, own_b, lib_in, lib_f, lib_b, power_f,
    mine, theirs, acc, x_out, x_in, y_own, y_out, y_in, z_own, z_f, z_out, z_in,
    local_sem, send_sem, recv_sem,
):
    x, yh, yl, z, core = place()
    y = yh * 4 + yl
    me = (x * 2 + yh) * 2 + core
    mate = 1 - core
    pair = device(x, y, z, mate)
    far = (y + 4) % 8
    base = core * 9
    send_slots, recv_slots = iter(range(200)), iter(range(200))

    def remote(src, dst, target, recv=None):
        recv = next(recv_slots) if recv is None else recv
        return pltpu.make_async_remote_copy(
            src_ref=src, dst_ref=dst, send_sem=send_sem.at[next(send_slots)], recv_sem=recv_sem.at[recv],
            device_id=target, device_id_type=MESH,
        )

    def arrival(dst, recv):
        return pltpu.make_async_remote_copy(
            src_ref=dst, dst_ref=dst, send_sem=send_sem.at[0], recv_sem=recv_sem.at[recv],
            device_id=pair, device_id_type=MESH,
        )

    sources = [device((x + d) % 4, y, z, c) for d in (1, 2, 3) for c in (0, 1)]
    sources += [device(x, far, z, mate)]
    sources += [device(x, (y + d) % 8, z, core) for d in range(1, 8)]
    sources += [device(x, y, (z + d) % 8, z // 4) for d in range(1, 8)]
    barrier = pltpu.get_barrier_semaphore()
    pl.semaphore_signal(barrier, inc=1, device_id=pair, device_id_type=MESH)
    for source in sources:
        pl.semaphore_signal(barrier, inc=1, device_id=source, device_id_type=MESH)
    copies = [
        pltpu.make_async_copy(src, dst, local_sem.at[k])
        for k, (src, dst) in enumerate((
            (proj_hbm, proj), (classes_hbm, classes_v), (precision_hbm, precision_v), (counts_hbm, counts_v),
            (shifts_hbm, shifts_v), (ctf_hbm, ctf), (img_hbm, img.at[core]),
        ))
    ]
    for copy in copies:
        copy.start()

    copies[0].wait()
    own_f[...] = proj[...].astype(F32)
    for h in range(2):
        for q in range(4):
            for p in range(2):
                for c in range(2):
                    rows = own_f[pl.ds(p * RAW + 36 * q + 18 * h + c, 9, stride=2), :]
                    own_r[pl.ds(h * BLOCK + 36 * q + 2 * c + p, 9, stride=4), :] = rows
    own_b[0] = own_r[0:BLOCK, :].astype(BF16)
    own_b[1] = own_r[BLOCK:2 * BLOCK, :].astype(BF16)
    lib_in[me] = own_b[core]

    for copy in copies[1:4]:
        copy.wait()

    def column_of(row, size):
        r = lax.broadcasted_iota(jnp.int32, (size, row.shape[1]), 0)
        c = lax.broadcasted_iota(jnp.int32, (size, row.shape[1]), 1)
        return jnp.sum(jnp.where(r == c, jnp.broadcast_to(row, r.shape), 0.0), axis=1, keepdims=True)

    lane24 = lax.broadcasted_iota(jnp.int32, (CAP, 128), 1)
    alive = lax.broadcasted_iota(jnp.int32, (CAP, 1), 0) < counts_v[...]
    meta[core] = jnp.where(
        lane24 == 0, column_of(classes_v[...].astype(F32), CAP),
        jnp.where(lane24 == 1, column_of(precision_v[...], CAP), jnp.where(alive, 1.0, 0.0)),
    )
    pl.semaphore_wait(barrier, 15 + jnp.where(z // 4 == core, 6, 8))

    sent = []
    meta_copy = remote(meta.at[core], meta.at[core], pair)
    block_copy = remote(own_b.at[mate], lib_in.at[me], pair)
    img_copy = remote(img_hbm, img.at[core], pair)
    targets = [(x, far)] + [((x + d) % 4, y) for d in (1, 3, 2)]
    first_slots = []
    for first, count in LIB_CHUNKS:
        rows = pl.ds(first * 4, count * 4)
        slots = []
        for px, py in targets:
            pick = [next(recv_slots), next(recv_slots)]
            slots.append(pick)
            for h in range(2):
                copy = remote(
                    own_b.at[h, rows], lib_in.at[me, rows], device(px, py, z, h), pick[0] + core
                )
                copy.start()
                sent.append(copy)
        first_slots.append(slots)
    for copy in (meta_copy, block_copy, img_copy):
        copy.start()
        sent.append(copy)

    copies[4].wait()
    step = shifts_v[...].astype(F32)
    step_x = jnp.broadcast_to(column_of(step[0:1, :], 16), (16, 128))
    step_y = jnp.broadcast_to(column_of(step[1:2, :], 16), (16, 128))
    fine = []
    lanes = lax.broadcasted_iota(jnp.int32, (16, 128), 1)
    for u in range(3):
        j = lanes + u * 128
        dy = (j >= 96).astype(jnp.int32) + (j >= 192).astype(jnp.int32) + (j >= 288).astype(jnp.int32)
        kx = j - 96 * dy
        angle = STEP * (step_x * kx.astype(F32) + step_y * dy.astype(F32))
        fine.append((jnp.cos(angle), jnp.sin(angle)))
    start = STEP * (step_y * (12 * core - FREQ // 2).astype(F32))
    turn = STEP * (step_y * 4.0)
    leap = STEP * (step_y * 16.0)
    turn_c, turn_s, leap_c, leap_s = jnp.cos(turn), jnp.sin(turn), jnp.cos(leap), jnp.sin(leap)
    phase = (jnp.cos(start), jnp.sin(start))

    copies[5].wait()
    arrival(meta.at[mate], 0).wait_recv()
    both = jnp.concatenate([meta[0], meta[1]], axis=0)
    klass, prec, live = both[:, 0:1], both[:, 1:2], both[:, 2:3]
    kinds = lax.broadcasted_iota(jnp.int32, (PAIR, CLASSES), 1).astype(F32)
    onehot = (klass == kinds).astype(F32)
    pick = jnp.concatenate([onehot, onehot, onehot], axis=1).astype(BF16)
    for q in range(4):
        c = ctf[:, pl.ds(pl.multiple_of((18 * q + base) * 128, 128), 1152)]
        hi = c.astype(BF16).astype(F32)
        mid = (c - hi).astype(BF16).astype(F32)
        low = c - hi - mid
        parts = jnp.concatenate([hi, mid, low], axis=0).astype(BF16)
        crow[:, q * 1152:(q + 1) * 1152] = jnp.dot(pick, parts, preferred_element_type=F32)

    def widen(n, carry):
        for c in range(2):
            src = pl.ds(pl.multiple_of(n * RAW, 16), RAW)
            raw[pl.ds(pl.multiple_of((c * CAP + n) * RAW, 16), RAW), :] = img[c, src, :].astype(F32)
        return carry

    copies[6].wait()
    arrival(img.at[mate], 2).wait_recv()
    lax.fori_loop(0, CAP, widen, 0)

    def shift_tiles(i, carry):
        base_c, base_s = carry
        q, v = i // 3, i % 3
        for u in range(3):
            t = 18 * q + base + 3 * v + u
            tt = 3 * i + u
            fc, fs = fine[u]
            cosine = fc * base_c - fs * base_s
            sine = fs * base_c + fc * base_s
            c_tile = crow[:, pl.ds(pl.multiple_of(tt * 128, 128), 128)]
            real, imag = [], []
            for g in range(6):
                c = c_tile[8 * g:8 * g + 8, :]
                real.append(raw[pl.ds(g * 8 * RAW + 2 * t, 8, stride=RAW), :] * c)
                imag.append(raw[pl.ds(g * 8 * RAW + 2 * t + 1, 8, stride=RAW), :] * c)
            re_s, im_s, re_b, im_b = [], [], [], []
            for s in range(SHIFTS):
                cs = jnp.broadcast_to(cosine[s:s + 1, :], (8, 128))
                sn = jnp.broadcast_to(sine[s:s + 1, :], (8, 128))
                for g in range(6):
                    ac, bs = real[g] * cs, imag[g] * sn
                    bc, as_ = imag[g] * cs, real[g] * sn
                    re_s.append(ac + bs)
                    im_s.append(bc - as_)
                    re_b.append(ac - bs)
                    im_b.append(bc + as_)
            for dst, parts in ((shifted, (re_s, im_s)), (back, (re_b, im_b))):
                for k, part in enumerate(parts):
                    cols = pl.ds(pl.multiple_of(tt * 256 + k * 128, 128), 128)
                    dst[:, cols] = jnp.concatenate(part, axis=0).astype(BF16)
        last = v == 2
        tc, ts = jnp.where(last, leap_c, turn_c), jnp.where(last, leap_s, turn_s)
        return base_c * tc - base_s * ts, base_s * tc + base_c * ts

    other = (x * 2 + 1 - yh) * 2
    second_slots = []

    def hand_on(chunk):
        first, count = LIB_CHUNKS[chunk]
        rows = pl.ds(first * 4, count * 4)
        for k in range(2):
            arrival(lib_in.at[other + k, rows], first_slots[chunk][0][k]).wait_recv()
        slots = []
        view = lib_in.at[pl.ds(other, 2), rows]
        for d in (1, 3, 2):
            copy = remote(view, view, device((x + d) % 4, y, z, core))
            copy.start()
            sent.append(copy)
            slots.append(copy)
        second_slots.append(slots)

    phase = lax.fori_loop(0, 3, shift_tiles, phase)
    hand_on(0)
    phase = lax.fori_loop(3, 6, shift_tiles, phase)
    hand_on(1)
    phase = lax.fori_loop(6, 12, shift_tiles, phase)

    powers = jnp.zeros((CLASSES, POSES), F32)
    total = jnp.zeros((ROWS, POSES), F32)
    arrival(lib_in.at[0], 1).wait_recv()
    for chunk, (first, count) in enumerate(LIB_CHUNKS):
        rows = pl.ds(first * 4, count * 4)
        for pick_slots in first_slots[chunk][1:]:
            for slot in pick_slots:
                arrival(lib_in.at[0, rows], slot).wait_recv()
        for copy in second_slots[chunk]:
            copy.wait_recv()

        def widen_lib(k, carry):
            lib_f[pl.ds(pl.multiple_of(k * BLOCK + first * 4, 16), count * 4), :] = lib_in[k, rows, :].astype(F32)
            return carry

        lax.fori_loop(0, 16, widen_lib, 0)

        def gather_tiles(i, carry):
            for u in range(4):
                tt = first + i * 4 + u
                halves = []
                for k in range(2):
                    parts = [
                        lib_f[pl.ds(c * BLOCK + tt * 4 + k * 2 + p, 8, stride=2 * BLOCK), :]
                        for c in range(2) for p in range(2)
                    ]
                    halves.append(jnp.concatenate(parts, axis=0))
                cols = pl.ds(pl.multiple_of(tt * 256, 256), 256)
                lib_b[:, cols] = jnp.concatenate(halves, axis=1).astype(BF16)
                cols = pl.ds(pl.multiple_of(tt * 128, 128), 128)
                power_f[:, cols] = halves[0] * halves[0] + halves[1] * halves[1]
            return carry

        lax.fori_loop(0, count // 4, gather_tiles, 0)
        for q in range(4):
            lo, hi = max(first, 9 * q), min(first + count, 9 * q + 9)
            if lo < hi:
                c = ctf[:, pl.ds(pl.multiple_of((9 * q + base + lo) * 128, 128), (hi - lo) * 128)]
                powers = powers + lax.dot_general(
                    c * c, power_f[:, lo * 128:hi * 128], (((1,), (1,)), ((), ())),
                    precision=lax.Precision.HIGHEST, preferred_element_type=F32,
                )
        cols = slice(first * 256, (first + count) * 256)
        total = total + lax.dot_general(
            shifted[:, cols], lib_b[:, cols], (((1,), (1,)), ((), ())), preferred_element_type=F32
        )
    class_power = jnp.zeros((PAIR, POSES), F32)
    for k in range(CLASSES):
        class_power = class_power + jnp.where(klass == float(k), powers[k:k + 1, :], 0.0)
    parts = [total[s * PAIR:(s + 1) * PAIR, :] - 0.5 * class_power for s in range(SHIFTS)]
    for s in range(SHIFTS):
        mine[s * PAIR:(s + 1) * PAIR, 0:POSES] = parts[s]
    score_copy = remote(mine, theirs, pair)
    score_copy.start()
    sent.append(score_copy)
    for g in range(32):
        acc[pl.ds(g * UNIT + 72, 8), :] = jnp.zeros((8, 128), F32)
    score_copy.wait_recv()
    scores = [prec * (parts[s] + theirs[s * PAIR:(s + 1) * PAIR, 0:POSES]) for s in range(SHIFTS)]
    top = scores[0]
    for s in range(1, SHIFTS):
        top = jnp.maximum(top, scores[s])
    top = jnp.max(top, axis=1, keepdims=True)
    mass = jnp.exp(scores[0] - top)
    for s in range(1, SHIFTS):
        mass = mass + jnp.exp(scores[s] - top)
    log_norm = top + jnp.log(jnp.sum(mass, axis=1, keepdims=True))
    weight = jnp.concatenate([jnp.where(live > 0.5, jnp.exp(v - log_norm), 0.0) for v in scores], axis=0).astype(BF16)
    unit = lax.broadcasted_iota(jnp.int32, (POSES, POSES), 0) == lax.broadcasted_iota(jnp.int32, (POSES, POSES), 1)
    weight_t = lax.dot_general(
        unit.astype(F32).astype(BF16), weight, (((1,), (1,)), ((), ())), preferred_element_type=F32
    ).astype(BF16)

    x_sends = []
    for first, count, low, high in CHUNKS:
        rows = pl.ds(low, high - low)

        def sum_quarter(q, carry):
            cols = pl.ds(pl.multiple_of((q * 9 + first) * 256, 256), count * 256)
            part = jnp.dot(weight_t, back[:, cols], preferred_element_type=F32)
            for c in range(2):
                for p in range(2):
                    r = c * 16 + p * 8
                    for k in range(2 * count):
                        row = q * UNIT + first * 8 + (k // 2) * 8 + c * 4 + (k % 2) * 2 + p
                        acc[pl.ds(row, 8, stride=4 * UNIT), :] = part[r:r + 8, k * 128:(k + 1) * 128]
            for d in range(1, 4):
                for h in range(2):
                    at = pl.multiple_of((((x + d) % 4 * 2 + h) * 4 + q) * UNIT + low, 16)
                    x_out[d - 1, h, q, rows, :] = acc[pl.ds(at, high - low), :].astype(BF16)
            return carry

        lax.fori_loop(0, 4, sum_quarter, 0)
        chunk_sends = []
        for d in (2, 1, 3):
            copy = remote(
                x_out.at[d - 1, :, :, rows], x_in.at[d - 1, :, :, rows], device((x + d) % 4, y, z, core)
            )
            copy.start()
            chunk_sends.append(copy)
        x_sends.append(chunk_sends)
        sent += chunk_sends
    shown = jnp.where(live > 0.5, log_norm, 0.0)
    shown = jnp.where(core == 0, shown[0:CAP, :], shown[CAP:PAIR, :])
    r24 = lax.broadcasted_iota(jnp.int32, (CAP, 128), 0)
    norm_ref[...] = jnp.sum(jnp.where(r24 == lane24, shown, 0.0), axis=0, keepdims=True)

    y_sends = []
    for (first, count, low, high), chunk_sends in zip(CHUNKS, x_sends):
        rows = pl.ds(low, high - low)
        for copy in chunk_sends:
            copy.wait_recv()
        for h in range(2):
            for q in range(4):
                at = pl.multiple_of(((x * 2 + h) * 4 + q) * UNIT + low, 16)
                part = acc[pl.ds(at, high - low), :]
                for d in range(3):
                    part = part + x_in[d, h, q, rows, :].astype(F32)
                y_own[h * 4 + q, rows, :] = part
                y_out[h * 4 + q, rows, :] = part.astype(BF16)
        chunk_sends = []
        for d in (4, 3, 5, 2, 6, 1, 7):
            py = (y + d) % 8
            copy = remote(y_out.at[py, rows], y_in.at[d - 1, rows], device(x, py, z, core))
            copy.start()
            chunk_sends.append(copy)
        y_sends.append(chunk_sends)
        sent += chunk_sends
    for (first, count, low, high), chunk_sends in zip(CHUNKS, y_sends):
        rows = pl.ds(low, high - low)
        for copy in chunk_sends:
            copy.wait_recv()
        part = y_own[y, rows, :]
        for d in range(7):
            part = part + y_in[d, rows, :].astype(F32)
        z_own[rows, :] = part

    zeros4 = jnp.zeros((4, 128), F32)
    for k in range(4):
        for c in range(2):
            for i in range(3):
                first = (2 * k + i) * 8 + c * 4
                z_f[2 * k + c, 4 * i:4 * i + 4, :] = z_own[first:first + 4, :]
            z_f[2 * k + c, 12:16, :] = zeros4
            z_out[2 * k + c] = z_f[2 * k + c].astype(BF16)
    z_first = next(recv_slots)
    for _ in range(7):
        next(recv_slots)
    own_place = z // 4 == core
    z_sends = []
    for d in (2, 1, 3, 0):
        k = (z + d) % 4
        for c in (mate, core):
            z_sends.append(remote(
                z_out.at[2 * k + c], z_in.at[z], device(x, y, 4 * core + k, c), z_first + z
            ))
    for copy in z_sends[:-1]:
        copy.start()
    sent += z_sends[:-1]

    @pl.when(own_place)
    def _():
        z_in[z] = z_out[2 * (z % 4) + core]

    @pl.when(jnp.logical_not(own_place))
    def _():
        z_sends[-1].start()

    for k in range(8):
        @pl.when(jnp.logical_not(jnp.logical_and(own_place, z == k)))
        def _():
            arrival(z_in.at[k], z_first + k).wait_recv()

    part = z_in[0].astype(F32)
    for k in range(1, 8):
        part = part + z_in[k].astype(F32)
    skip = (z % 4) * 32
    turned = pltpu.roll(part, (128 - skip) % 128, 1)
    keep = lax.broadcasted_iota(jnp.int32, (4, 128), 1) < 128 - skip
    for t in range(3):
        piece = turned[4 * t:4 * t + 4, :]
        if t < 2:
            piece = jnp.where(keep, piece, turned[4 * t + 4:4 * t + 8, :])
        width = 128 if t < 2 else 32
        for p in range(2):
            for c in range(2):
                accum_ref[p, c:c + 1, t * 128:t * 128 + width] = piece[c * 2 + p:c * 2 + p + 1, 0:width]

    for copy in sent:
        copy.wait_send()

    @pl.when(jnp.logical_not(own_place))
    def _():
        z_sends[-1].wait_send()


def body(images, classes, precision, counts, shifts, ctf_table, projections):
    raw_img = images.reshape(CAP, 2, TILES, 128).transpose(0, 2, 1, 3).reshape(CAP * RAW, 128)
    raw_proj = projections.reshape(2, 2, TILES, 128).transpose(0, 2, 1, 3).reshape(2 * RAW, 128)
    vmem = pl.BlockSpec(memory_space=pltpu.VMEM)
    anywhere = pl.BlockSpec(memory_space=pl.ANY)
    accum, norm = pl.pallas_call(
        kernel,
        out_shape=(
            jax.ShapeDtypeStruct((2, 2, HALF // 32), F32),
            jax.ShapeDtypeStruct((1, 128), F32),
        ),
        in_specs=[anywhere] * 7,
        out_specs=(vmem, vmem),
        scratch_shapes=[
            pltpu.VMEM((1, CAP), jnp.int32),
            pltpu.VMEM((1, CAP), F32),
            pltpu.VMEM((1, 1), jnp.int32),
            pltpu.VMEM((2, SHIFTS), jnp.int32),
            pltpu.VMEM((2 * RAW, 128), BF16),
            pltpu.VMEM((2, CAP * RAW, 128), BF16),
            pltpu.VMEM((CLASSES, HALF), F32),
            pltpu.VMEM((PAIR * RAW, 128), F32),
            pltpu.VMEM((PAIR, HALF // 2), F32),
            pltpu.VMEM((ROWS, HALF), BF16),
            pltpu.VMEM((ROWS, HALF), BF16),
            pltpu.VMEM((2, CAP, 128), F32),
            pltpu.VMEM((2 * RAW, 128), F32),
            pltpu.VMEM((2 * BLOCK, 128), F32),
            pltpu.VMEM((2, BLOCK, 128), BF16),
            pltpu.VMEM((16, BLOCK, 128), BF16),
            pltpu.VMEM((16 * BLOCK, 128), F32),
            pltpu.VMEM((POSES, HALF), BF16),
            pltpu.VMEM((POSES, HALF // 2), F32),
            pltpu.VMEM((ROWS, 128), F32),
            pltpu.VMEM((ROWS, 128), F32),
            pltpu.VMEM((32 * UNIT, 128), F32),
            pltpu.VMEM((3, 2, 4, UNIT, 128), BF16),
            pltpu.VMEM((3, 2, 4, UNIT, 128), BF16),
            pltpu.VMEM((8, UNIT, 128), F32),
            pltpu.VMEM((8, UNIT, 128), BF16),
            pltpu.VMEM((7, UNIT, 128), BF16),
            pltpu.VMEM((UNIT, 128), F32),
            pltpu.VMEM((8, 16, 128), F32),
            pltpu.VMEM((8, 16, 128), BF16),
            pltpu.VMEM((8, 16, 128), BF16),
            pltpu.SemaphoreType.DMA((7,)),
            pltpu.SemaphoreType.DMA((80,)),
            pltpu.SemaphoreType.DMA((80,)),
        ],
        compiler_params=pltpu.CompilerParams(
            collective_id=0, has_side_effects=True, vmem_limit_bytes=56 * 1024 * 1024
        ),
        name="expectation",
    )(
        classes.reshape(1, CAP), precision.reshape(1, CAP), counts.reshape(1, 1), shifts.T,
        raw_img, ctf_table, raw_proj,
    )
    return accum, norm.reshape(128)[:CAP]


def solution(mesh):
    placed = (
        P(("lib", "dom"), None, None),
        P(("lib", "dom")),
        P(("lib", "dom")),
        P(("lib", "dom")),
        P(),
        P(),
        P("lib", None, None),
    )
    return jax.shard_map(
        body,
        mesh=mesh,
        in_specs=placed,
        out_specs=(P("lib", None, "dom"), P(("lib", "dom"))),
        check_vma=False,
    )
```

```python
import functools
import math

import jax
import jax.numpy as jnp
import numpy as np
from jax import lax
from jax.experimental import pallas as pl
from jax.experimental.pallas import tpu as pltpu
from jax.sharding import PartitionSpec as P

FREQ = 96
SHIFTS = 9
HALF = 9216
CLASSES = 8
CAP = 24
POSES = 32
TILES = 72
RAW = 2 * TILES
WIDE = 2 * HALF
ROWS = SHIFTS * CAP + 8
HALF_TILES = TILES // 2
BLOCK = HALF_TILES * 4
LIB_CHUNKS = ((0, 12), (12, 12), (24, 12))
STEP = 2.0 * np.pi / (2.0 * FREQ)
CHUNKS = ((0, 2), (2, 2), (4, 2), (6, 2), (8, 1))
MESH = pl.DeviceIdType.MESH
F32 = jnp.float32
BF16 = jnp.bfloat16


def place():
    lib = lax.axis_index("lib")
    dom = lax.axis_index("dom")
    return lib // 4, (lib // 2) % 2, dom // 8, dom % 8, lib % 2


def device(x, y, z, core):
    return ((x * 2 + y // 4) * 2 + core, (y % 4) * 8 + z)


def kernel(
    classes_hbm, precision_hbm, counts_hbm, shifts_hbm, img_hbm, ctf_hbm, proj_hbm,
    accum_ref, norm_ref,
    classes_v, precision_v, counts_v, shifts_v, proj,
    img, ctf, raw, crow, phases, shifted, back, meta, own_f, own_r, own_b, lib_in, lib_f, lib_b, power_f,
    mine, theirs, acc, x_out, x_in, y_own, y_out, y_in, z_own, z_f, z_out, z_in,
    local_sem, send_sem, recv_sem,
):
    x, yh, yl, z, core = place()
    y = yh * 4 + yl
    me = (x * 2 + yh) * 2 + core
    mate = 1 - core
    pair = device(x, y, z, mate)
    edge = jnp.logical_or(yl == 0, yl == 3)
    near = jnp.where(yl < 2, y + 7 - yl, y + 4 - yl) % 8
    beyond = [jnp.where(yl == 0, y + 7 - k, y + 1 + k) % 8 for k in range(2)]
    base = core * 9
    send_slots, recv_slots = iter(range(200)), iter(range(200))

    def remote(src, dst, target, recv=None):
        recv = next(recv_slots) if recv is None else recv
        return pltpu.make_async_remote_copy(
            src_ref=src, dst_ref=dst, send_sem=send_sem.at[next(send_slots)], recv_sem=recv_sem.at[recv],
            device_id=target, device_id_type=MESH,
        )

    def arrival(dst, recv):
        return pltpu.make_async_remote_copy(
            src_ref=dst, dst_ref=dst, send_sem=send_sem.at[0], recv_sem=recv_sem.at[recv],
            device_id=pair, device_id_type=MESH,
        )

    sources = [device((x + d) % 4, y, z, c) for d in (1, 2, 3) for c in (0, 1)]
    sources += [device(x, near, z, mate)]
    sources += [device(x, (y + d) % 8, z, core) for d in range(1, 8)]
    sources += [device(x, y, (z + d) % 8, z // 4) for d in range(1, 8)]
    barrier = pltpu.get_barrier_semaphore()
    pl.semaphore_signal(barrier, inc=1, device_id=pair, device_id_type=MESH)
    for source in sources:
        pl.semaphore_signal(barrier, inc=1, device_id=source, device_id_type=MESH)
    copies = [
        pltpu.make_async_copy(src, dst, local_sem.at[k])
        for k, (src, dst) in enumerate((
            (proj_hbm, proj), (classes_hbm, classes_v), (precision_hbm, precision_v), (counts_hbm, counts_v),
            (shifts_hbm, shifts_v), (ctf_hbm, ctf), (img_hbm, img.at[core]),
        ))
    ]
    for copy in copies:
        copy.start()

    def column_of(row, size):
        r = lax.broadcasted_iota(jnp.int32, (size, row.shape[1]), 0)
        c = lax.broadcasted_iota(jnp.int32, (size, row.shape[1]), 1)
        return jnp.sum(jnp.where(r == c, jnp.broadcast_to(row, r.shape), 0.0), axis=1, keepdims=True)

    copies[0].wait()
    own_f[...] = proj[...].astype(F32)
    for h in range(2):
        for q in range(4):
            for p in range(2):
                for c in range(2):
                    rows = own_f[pl.ds(p * RAW + 36 * q + 18 * h + c, 9, stride=2), :]
                    own_r[pl.ds(h * BLOCK + 36 * q + 2 * c + p, 9, stride=4), :] = rows
    own_b[0] = own_r[0:BLOCK, :].astype(BF16)
    own_b[1] = own_r[BLOCK:2 * BLOCK, :].astype(BF16)
    lib_in[me] = own_b[core]

    pl.semaphore_wait(barrier, 14 + jnp.where(z // 4 == core, 6, 8) + jnp.where(edge, 2, 0))

    sent = []
    meta_copy = remote(meta.at[core], meta.at[core], pair)
    block_copy = remote(own_b.at[mate], lib_in.at[me], pair)
    img_copy = remote(img_hbm, img.at[core], pair)
    far_sends, far_slots, first_slots, second_slots = [], [], [], []
    for first, count in LIB_CHUNKS:
        rows = pl.ds(first * 4, count * 4)
        pick = [next(recv_slots), next(recv_slots)]
        far_slots.append(pick)
        for py in (beyond[1], beyond[0]):
            for h in range(2):
                far_sends.append(
                    remote(own_b.at[h, rows], lib_in.at[me, rows], device(x, py, z, h), pick[0] + core)
                )

    @pl.when(edge)
    def _():
        for copy in far_sends:
            copy.start()

    for first, count in LIB_CHUNKS:
        rows = pl.ds(first * 4, count * 4)
        for d in (2, 1, 3):
            pick = [next(recv_slots), next(recv_slots)]
            first_slots.append(pick)
            for h in range(2):
                copy = remote(
                    own_b.at[h, rows], lib_in.at[me, rows], device((x + d) % 4, y, z, h), pick[0] + core
                )
                copy.start()
                sent.append(copy)
    for copy in (block_copy, img_copy):
        copy.start()
        sent.append(copy)

    for copy in copies[1:4]:
        copy.wait()

    lane24 = lax.broadcasted_iota(jnp.int32, (CAP, 128), 1)
    alive = lax.broadcasted_iota(jnp.int32, (CAP, 1), 0) < counts_v[...]
    meta[core] = jnp.where(
        lane24 == 0, column_of(classes_v[...].astype(F32), CAP),
        jnp.where(lane24 == 1, column_of(precision_v[...], CAP), jnp.where(alive, 1.0, 0.0)),
    )
    def prepare(who):
        klass = meta[who][:, 0:1]
        kinds = lax.broadcasted_iota(jnp.int32, (CAP, CLASSES), 1).astype(F32)
        onehot = (klass == kinds).astype(F32)
        pick = jnp.concatenate([onehot, onehot, onehot], axis=1).astype(BF16)
        for q in range(4):
            c = ctf[:, pl.ds(pl.multiple_of((18 * q + base) * 128, 128), 1152)]
            hi = c.astype(BF16).astype(F32)
            mid = (c - hi).astype(BF16).astype(F32)
            low = c - hi - mid
            parts = jnp.concatenate([hi, mid, low], axis=0).astype(BF16)
            crow[:, q * 1152:(q + 1) * 1152] = jnp.dot(pick, parts, preferred_element_type=F32)

        def widen(n, carry):
            rows = pl.ds(pl.multiple_of(n * RAW, 16), RAW)
            raw[rows, :] = img[who, rows, :].astype(F32)
            return carry

        lax.fori_loop(0, CAP, widen, 0)

    zeros8 = jnp.zeros((8, 128), F32)

    def shift_tiles(who, i, carry):
        q, v = i // 3, i % 3
        for u in range(3):
            t = 18 * q + base + 3 * v + u
            tt = 3 * i + u
            cols = pl.ds(pl.multiple_of(tt * 128, 128), 128)
            real, imag = [], []
            for g in range(3):
                c = crow[8 * g:8 * g + 8, cols]
                real.append(raw[pl.ds(g * 8 * RAW + 2 * t, 8, stride=RAW), :] * c)
                imag.append(raw[pl.ds(g * 8 * RAW + 2 * t + 1, 8, stride=RAW), :] * c)
            pairs = []
            for k in range(SHIFTS * 3 + 1):
                s, g = k // 3, k % 3
                if s < SHIFTS:
                    if g == 0:
                        cs = jnp.broadcast_to(phases[0, pl.ds(s, 1), cols], (8, 128))
                        sn = jnp.broadcast_to(phases[1, pl.ds(s, 1), cols], (8, 128))
                    ac, bs = real[g] * cs, imag[g] * sn
                    bc, as_ = imag[g] * cs, real[g] * sn
                    pairs.append((ac + bs, bc - as_, ac - bs, bc + as_))
                else:
                    pairs.append((zeros8,) * 4)
                if k % 2:
                    for j, (dst, half) in enumerate(((shifted, 0), (shifted, 1), (back, 0), (back, 1))):
                        wide = pl.ds(pl.multiple_of(tt * 256 + half * 128, 128), 128)
                        both = jnp.concatenate([pairs[0][j], pairs[1][j]], axis=0).astype(BF16)
                        dst[who, pl.ds(8 * (k - 1), 16), wide] = both
                    pairs = []
        return carry

    meta_copy.start()
    sent.append(meta_copy)


    copies[4].wait()
    step = shifts_v[...].astype(F32)
    step_x = jnp.broadcast_to(column_of(step[0:1, :], 16), (16, 128))
    step_y = jnp.broadcast_to(column_of(step[1:2, :], 16), (16, 128))
    fine = []
    lanes = lax.broadcasted_iota(jnp.int32, (16, 128), 1)

    def turned_by(steps):
        steps = steps - 192.0 * jnp.floor(steps * (1.0 / 192.0) + 0.5)
        h = steps * (0.5 * STEP)
        h2 = h * h
        sn, cs = jnp.zeros_like(h), jnp.zeros_like(h)
        for k in range(7, -1, -1):
            sn = sn * h2 + (-1.0) ** k / math.factorial(2 * k + 1)
            cs = cs * h2 + (-1.0) ** k / math.factorial(2 * k)
        sn = sn * h
        return 1.0 - 2.0 * (sn * sn), 2.0 * (sn * cs)

    for u in range(3):
        j = lanes + u * 128
        dy = (j >= 96).astype(jnp.int32) + (j >= 192).astype(jnp.int32) + (j >= 288).astype(jnp.int32)
        kx = j - 96 * dy
        fine.append(turned_by(step_x * kx.astype(F32) + step_y * dy.astype(F32)))
    rows_on = jnp.where(lanes == 0, 12 * core - FREQ // 2, jnp.where(lanes == 1, 4, 16)).astype(F32)
    coarse = turned_by(step_y * rows_on)
    start_c, turn_c, leap_c = [jnp.broadcast_to(coarse[0][:, k:k + 1], (16, 128)) for k in range(3)]
    start_s, turn_s, leap_s = [jnp.broadcast_to(coarse[1][:, k:k + 1], (16, 128)) for k in range(3)]

    def table(i, carry):
        base_c, base_s = carry
        for u in range(3):
            fc, fs = fine[u]
            cols = pl.ds(pl.multiple_of((3 * i + u) * 128, 128), 128)
            phases[0, :, cols] = fc * base_c - fs * base_s
            phases[1, :, cols] = fs * base_c + fc * base_s
        last = i % 3 == 2
        tc, ts = jnp.where(last, leap_c, turn_c), jnp.where(last, leap_s, turn_s)
        return base_c * tc - base_s * ts, base_s * tc + base_c * ts

    lax.fori_loop(0, 12, table, (start_c, start_s))

    copies[5].wait()
    copies[6].wait()
    prepare(core)

    other = (x * 2 + 1 - yh) * 2

    def hand_on(chunk):
        first, count = LIB_CHUNKS[chunk]
        rows = pl.ds(first * 4, count * 4)
        for k in range(2):
            arrival(lib_in.at[other + k, rows], far_slots[chunk][k]).wait_recv()
        slots = []
        view = lib_in.at[pl.ds(other, 2), rows]
        for d in (2, 1, 3):
            copy = remote(view, view, device((x + d) % 4, y, z, core))
            copy.start()
            sent.append(copy)
            slots.append(copy)
        second_slots.append(slots)

    lax.fori_loop(0, 12, functools.partial(shift_tiles, core), 0, unroll=2)

    hand_on(0)

    arrival(meta.at[mate], 0).wait_recv()
    arrival(img.at[mate], 2).wait_recv()
    prepare(mate)
    lax.fori_loop(0, 2, functools.partial(shift_tiles, mate), 0, unroll=2)
    hand_on(1)
    lax.fori_loop(2, 6, functools.partial(shift_tiles, mate), 0, unroll=2)
    hand_on(2)
    lax.fori_loop(6, 12, functools.partial(shift_tiles, mate), 0, unroll=2)

    powers = jnp.zeros((CLASSES, POSES), F32)
    total = [jnp.zeros((ROWS, POSES), F32)] * 2
    arrival(lib_in.at[0], 1).wait_recv()
    for chunk, (first, count) in enumerate(LIB_CHUNKS):
        rows = pl.ds(first * 4, count * 4)
        for pick in first_slots[3 * chunk:3 * chunk + 3]:
            for slot in pick:
                arrival(lib_in.at[0, rows], slot).wait_recv()
        for copy in second_slots[chunk]:
            copy.wait_recv()

        def widen_lib(k, carry):
            lib_f[pl.ds(pl.multiple_of(k * BLOCK + first * 4, 16), count * 4), :] = lib_in[k, rows, :].astype(F32)
            return carry

        lax.fori_loop(0, 16, widen_lib, 0)

        def gather_tiles(i, carry):
            for u in range(4):
                tt = first + i * 4 + u
                halves = []
                for k in range(2):
                    parts = [
                        lib_f[pl.ds(c * BLOCK + tt * 4 + k * 2 + p, 8, stride=2 * BLOCK), :]
                        for c in range(2) for p in range(2)
                    ]
                    halves.append(jnp.concatenate(parts, axis=0))
                cols = pl.ds(pl.multiple_of(tt * 256, 256), 256)
                lib_b[:, cols] = jnp.concatenate(halves, axis=1).astype(BF16)
                cols = pl.ds(pl.multiple_of(tt * 128, 128), 128)
                power_f[:, cols] = halves[0] * halves[0] + halves[1] * halves[1]
            return carry

        lax.fori_loop(0, count // 4, gather_tiles, 0)
        for q in range(4):
            lo, hi = max(first, 9 * q), min(first + count, 9 * q + 9)
            if lo < hi:
                c = ctf[:, pl.ds(pl.multiple_of((9 * q + base + lo) * 128, 128), (hi - lo) * 128)]
                powers = powers + lax.dot_general(
                    c * c, power_f[:, lo * 128:hi * 128], (((1,), (1,)), ((), ())),
                    precision=lax.Precision.HIGHEST, preferred_element_type=F32,
                )
        cols = slice(first * 256, (first + count) * 256)
        for c in range(2):
            total[c] = total[c] + lax.dot_general(
                shifted[c, :, cols], lib_b[:, cols], (((1,), (1,)), ((), ())), preferred_element_type=F32
            )
    klass = [meta[c][:, 0:1] for c in range(2)]
    parts = []
    for c in range(2):
        class_power = jnp.zeros((CAP, POSES), F32)
        for k in range(CLASSES):
            class_power = class_power + jnp.where(klass[c] == float(k), powers[k:k + 1, :], 0.0)
        parts.append([total[c][s * CAP:(s + 1) * CAP, :] - 0.5 * class_power for s in range(SHIFTS)])
        for s in range(SHIFTS):
            mine[c, s * CAP:(s + 1) * CAP, 0:POSES] = parts[c][s]
    score_copy = remote(mine, theirs, pair)
    score_copy.start()
    sent.append(score_copy)
    score_copy.wait_recv()
    log_norm, weights = [], []
    for c in range(2):
        prec, live = meta[c][:, 1:2], meta[c][:, 2:3] > 0.5
        scores = [prec * (parts[c][s] + theirs[c, s * CAP:(s + 1) * CAP, 0:POSES]) for s in range(SHIFTS)]
        top = scores[0]
        for s in range(1, SHIFTS):
            top = jnp.maximum(top, scores[s])
        top = jnp.max(top, axis=1, keepdims=True)
        mass = jnp.exp(scores[0] - top)
        for s in range(1, SHIFTS):
            mass = mass + jnp.exp(scores[s] - top)
        norm = top + jnp.log(jnp.sum(mass, axis=1, keepdims=True))
        log_norm.append(jnp.where(live, norm, 0.0))
        weights += [jnp.where(live, jnp.exp(v - norm), 0.0) for v in scores] + [jnp.zeros((8, POSES), F32)]
    weight = jnp.concatenate(weights, axis=0).astype(BF16)
    unit = lax.broadcasted_iota(jnp.int32, (POSES, POSES), 0) == lax.broadcasted_iota(jnp.int32, (POSES, POSES), 1)
    weight_t = lax.dot_general(
        unit.astype(F32).astype(BF16), weight, (((1,), (1,)), ((), ())), preferred_element_type=F32
    ).astype(BF16)

    x_sends = []
    for first, count in CHUNKS:
        rows = pl.ds(64 * first, 64 * count)

        def sum_quarter(q, carry):
            cols = pl.ds(pl.multiple_of((q * 9 + first) * 256, 256), count * 256)
            part = jnp.dot(weight_t[:, 0:ROWS], back[0, :, cols], preferred_element_type=F32)
            part = part + jnp.dot(weight_t[:, ROWS:2 * ROWS], back[1, :, cols], preferred_element_type=F32)
            for c in range(2):
                for p in range(2):
                    r = c * 16 + p * 8
                    for k in range(2 * count):
                        row = 256 * first + (q * count + k // 2) * 8 + c * 4 + (k % 2) * 2 + p
                        acc[pl.ds(row, 8, stride=32 * count), :] = part[r:r + 8, k * 128:(k + 1) * 128]
            return carry

        lax.fori_loop(0, 4, sum_quarter, 0)
        chunk_sends = []
        for d in (2, 1, 3):
            at = pl.multiple_of(256 * first + (x + d) % 4 * 64 * count, 64)
            x_out[d - 1, rows, :] = acc[pl.ds(at, 64 * count), :].astype(BF16)
            copy = remote(x_out.at[d - 1, rows], x_in.at[d - 1, rows], device((x + d) % 4, y, z, core))
            copy.start()
            chunk_sends.append(copy)
        x_sends.append(chunk_sends)
        sent += chunk_sends
    shown = jnp.where(core == 0, log_norm[0], log_norm[1])
    r24 = lax.broadcasted_iota(jnp.int32, (CAP, 128), 0)
    norm_ref[...] = jnp.sum(jnp.where(r24 == lane24, shown, 0.0), axis=0, keepdims=True)

    y_sends = []
    for (first, count), chunk_sends in zip(CHUNKS, x_sends):
        rows = pl.ds(64 * first, 64 * count)
        size = 8 * count
        for copy in chunk_sends:
            copy.wait_recv()
        part = acc[pl.ds(pl.multiple_of(256 * first + x * 64 * count, 64), 64 * count), :]
        for d in range(3):
            part = part + x_in[d, rows, :].astype(F32)
        room = pl.ds(8 * first, max(size, 16))
        for g in range(8):
            piece = part[g * size:(g + 1) * size, :]
            y_own[g, pl.ds(8 * first, size), :] = piece
            if size < 16:
                piece = jnp.concatenate([piece, zeros8], axis=0)
            y_out[g, room, :] = piece.astype(BF16)
        chunk_sends = []
        for d in (4, 3, 5, 2, 6, 1, 7):
            py = (y + d) % 8
            copy = remote(y_out.at[py, room], y_in.at[d - 1, room], device(x, py, z, core))
            copy.start()
            chunk_sends.append(copy)
        y_sends.append(chunk_sends)
        sent += chunk_sends
    for (first, count), chunk_sends in zip(CHUNKS, y_sends):
        size = 8 * count
        for copy in chunk_sends:
            copy.wait_recv()
        part = y_own[y, pl.ds(8 * first, size), :]
        for d in range(7):
            part = part + y_in[d, pl.ds(8 * first, max(size, 16)), :].astype(F32)[0:size, :]
        z_own[pl.ds(8 * first, size), :] = part

    zeros4 = jnp.zeros((4, 128), F32)
    for k in range(4):
        for c in range(2):
            for i in range(3):
                first = (2 * k + i) * 8 + c * 4
                z_f[2 * k + c, 4 * i:4 * i + 4, :] = z_own[first:first + 4, :]
            z_f[2 * k + c, 12:16, :] = zeros4
            z_out[2 * k + c] = z_f[2 * k + c].astype(BF16)
    z_first = next(recv_slots)
    for _ in range(7):
        next(recv_slots)
    own_place = z // 4 == core
    z_sends = []
    for d in (2, 1, 3, 0):
        k = (z + d) % 4
        for c in (mate, core):
            z_sends.append(remote(
                z_out.at[2 * k + c], z_in.at[z], device(x, y, 4 * core + k, c), z_first + z
            ))
    for copy in z_sends[:-1]:
        copy.start()
    sent += z_sends[:-1]

    @pl.when(own_place)
    def _():
        z_in[z] = z_out[2 * (z % 4) + core]

    @pl.when(jnp.logical_not(own_place))
    def _():
        z_sends[-1].start()

    for k in range(8):
        @pl.when(jnp.logical_not(jnp.logical_and(own_place, z == k)))
        def _():
            arrival(z_in.at[k], z_first + k).wait_recv()

    part = z_in[0].astype(F32)
    for k in range(1, 8):
        part = part + z_in[k].astype(F32)
    skip = (z % 4) * 32
    turned = pltpu.roll(part, (128 - skip) % 128, 1)
    keep = lax.broadcasted_iota(jnp.int32, (4, 128), 1) < 128 - skip
    for t in range(3):
        piece = turned[4 * t:4 * t + 4, :]
        if t < 2:
            piece = jnp.where(keep, piece, turned[4 * t + 4:4 * t + 8, :])
        for p in range(2):
            for c in range(2):
                accum_ref[p, c:c + 1, t * 128:t * 128 + 128] = piece[c * 2 + p:c * 2 + p + 1, :]

    for copy in sent:
        copy.wait_send()

    @pl.when(edge)
    def _():
        for copy in far_sends:
            copy.wait_send()

    @pl.when(jnp.logical_not(own_place))
    def _():
        z_sends[-1].wait_send()


def body(images, classes, precision, counts, shifts, ctf_table, projections):
    raw_img = images.reshape(CAP, 2, TILES, 128).transpose(0, 2, 1, 3).reshape(CAP * RAW, 128)
    raw_proj = projections.reshape(2, 2, TILES, 128).transpose(0, 2, 1, 3).reshape(2 * RAW, 128)
    vmem = pl.BlockSpec(memory_space=pltpu.VMEM)
    anywhere = pl.BlockSpec(memory_space=pl.ANY)
    accum, norm = pl.pallas_call(
        kernel,
        out_shape=(
            jax.ShapeDtypeStruct((2, 2, 384), F32),
            jax.ShapeDtypeStruct((1, 128), F32),
        ),
        in_specs=[anywhere] * 7,
        out_specs=(vmem, vmem),
        scratch_shapes=[
            pltpu.VMEM((1, CAP), jnp.int32),
            pltpu.VMEM((1, CAP), F32),
            pltpu.VMEM((1, 1), jnp.int32),
            pltpu.VMEM((2, SHIFTS), jnp.int32),
            pltpu.VMEM((2 * RAW, 128), BF16),
            pltpu.VMEM((2, CAP * RAW, 128), BF16),
            pltpu.VMEM((CLASSES, HALF), F32),
            pltpu.VMEM((CAP * RAW, 128), F32),
            pltpu.VMEM((CAP, HALF // 2), F32),
            pltpu.VMEM((2, 16, HALF // 2), F32),
            pltpu.VMEM((2, ROWS, HALF), BF16),
            pltpu.VMEM((2, ROWS, HALF), BF16),
            pltpu.VMEM((2, CAP, 128), F32),
            pltpu.VMEM((2 * RAW, 128), F32),
            pltpu.VMEM((2 * BLOCK, 128), F32),
            pltpu.VMEM((2, BLOCK, 128), BF16),
            pltpu.VMEM((16, BLOCK, 128), BF16),
            pltpu.VMEM((16 * BLOCK, 128), F32),
            pltpu.VMEM((POSES, HALF), BF16),
            pltpu.VMEM((POSES, HALF // 2), F32),
            pltpu.VMEM((2, ROWS, 128), F32),
            pltpu.VMEM((2, ROWS, 128), F32),
            pltpu.VMEM((32 * 72, 128), F32),
            pltpu.VMEM((3, 576, 128), BF16),
            pltpu.VMEM((3, 576, 128), BF16),
            pltpu.VMEM((8, 72, 128), F32),
            pltpu.VMEM((8, 80, 128), BF16),
            pltpu.VMEM((7, 80, 128), BF16),
            pltpu.VMEM((72, 128), F32),
            pltpu.VMEM((8, 16, 128), F32),
            pltpu.VMEM((8, 16, 128), BF16),
            pltpu.VMEM((8, 16, 128), BF16),
            pltpu.SemaphoreType.DMA((7,)),
            pltpu.SemaphoreType.DMA((128,)),
            pltpu.SemaphoreType.DMA((128,)),
        ],
        compiler_params=pltpu.CompilerParams(
            collective_id=0, has_side_effects=True, vmem_limit_bytes=56 * 1024 * 1024
        ),
        name="expectation",
    )(
        classes.reshape(1, CAP), precision.reshape(1, CAP), counts.reshape(1, 1), shifts.T,
        raw_img, ctf_table, raw_proj,
    )
    return accum[:, :, :HALF // 32], norm.reshape(128)[:CAP]


def solution(mesh):
    placed = (
        P(("lib", "dom"), None, None),
        P(("lib", "dom")),
        P(("lib", "dom")),
        P(("lib", "dom")),
        P(),
        P(),
        P("lib", None, None),
    )
    return jax.shard_map(
        body,
        mesh=mesh,
        in_specs=placed,
        out_specs=(P("lib", None, "dom"), P(("lib", "dom"))),
        check_vma=False,
    )
```

```python
import functools
import math

import jax
import jax.numpy as jnp
import numpy as np
from jax import lax
from jax.experimental import pallas as pl
from jax.experimental.pallas import tpu as pltpu
from jax.sharding import PartitionSpec as P

FREQ = 96
SHIFTS = 9
HALF = 9216
CLASSES = 8
CAP = 24
POSES = 32
TILES = 72
RAW = 2 * TILES
WIDE = 2 * HALF
ROWS = SHIFTS * CAP + 8
HALF_TILES = TILES // 2
BLOCK = HALF_TILES * 4
LIB_CHUNKS = ((0, 12, 48), (12, 12, 48), (24, 12, 64))
FULL = BLOCK + 16
STEP = 2.0 * np.pi / (2.0 * FREQ)
CHUNKS = ((2, 2), (4, 2), (6, 2), (8, 1))
LEAD = 2
MESH = pl.DeviceIdType.MESH
F32 = jnp.float32
BF16 = jnp.bfloat16


def place():
    lib = lax.axis_index("lib")
    dom = lax.axis_index("dom")
    return lib // 4, (lib // 2) % 2, dom // 8, dom % 8, lib % 2


def device(x, y, z, core):
    return ((x * 2 + y // 4) * 2 + core, (y % 4) * 8 + z)


def kernel(
    classes_hbm, precision_hbm, counts_hbm, shifts_hbm, img_hbm, ctf_hbm, proj_hbm,
    accum_ref, norm_ref,
    classes_v, precision_v, counts_v, shifts_v, proj,
    img, ctf, raw, crow, phases, shifted, back, meta, own_f, own_r, own_p, own_b, lib_in, lib_f, lib_b,
    mine, theirs, acc, x_out, x_in, y_own, y_out, y_in, lead_out, lead_in, last_own, last_out, last_in, z_own, z_f, z_out, z_in,
    local_sem, send_sem, recv_sem,
):
    x, yh, yl, z, core = place()
    y = yh * 4 + yl
    me = (x * 2 + yh) * 2 + core
    mate = 1 - core
    pair = device(x, y, z, mate)
    edge = jnp.logical_or(yl == 0, yl == 3)
    near = jnp.where(yl < 2, y + 7 - yl, y + 4 - yl) % 8
    beyond = [jnp.where(yl == 0, y + 7 - k, y + 1 + k) % 8 for k in range(2)]
    base = core * 9
    send_slots, recv_slots = iter(range(200)), iter(range(200))

    def remote(src, dst, target, recv=None):
        recv = next(recv_slots) if recv is None else recv
        return pltpu.make_async_remote_copy(
            src_ref=src, dst_ref=dst, send_sem=send_sem.at[next(send_slots)], recv_sem=recv_sem.at[recv],
            device_id=target, device_id_type=MESH,
        )

    def arrival(dst, recv):
        return pltpu.make_async_remote_copy(
            src_ref=dst, dst_ref=dst, send_sem=send_sem.at[0], recv_sem=recv_sem.at[recv],
            device_id=pair, device_id_type=MESH,
        )

    copies = [
        pltpu.make_async_copy(src, dst, local_sem.at[k])
        for k, (src, dst) in enumerate((
            (proj_hbm, proj), (classes_hbm, classes_v), (precision_hbm, precision_v), (counts_hbm, counts_v),
            (shifts_hbm, shifts_v), (ctf_hbm, ctf), (img_hbm, img.at[core]),
        ))
    ]
    copies[0].start()

    sources = [device((x + d) % 4, y, z, c) for d in (1, 2, 3) for c in (0, 1)]
    sources += [device(x, near, z, mate)]
    sources += [device(x, (y + d) % 8, z, core) for d in range(1, 8)]
    sources += [device(x, y, (z + d) % 8, z // 4) for d in range(1, 8)]
    barrier = pltpu.get_barrier_semaphore()
    pl.semaphore_signal(barrier, inc=1, device_id=pair, device_id_type=MESH)
    for source in sources:
        pl.semaphore_signal(barrier, inc=1, device_id=source, device_id_type=MESH)
    for copy in copies[1:]:
        copy.start()

    def column_of(row, size):
        r = lax.broadcasted_iota(jnp.int32, (size, row.shape[1]), 0)
        c = lax.broadcasted_iota(jnp.int32, (size, row.shape[1]), 1)
        return jnp.sum(jnp.where(r == c, jnp.broadcast_to(row, r.shape), 0.0), axis=1, keepdims=True)

    copies[0].wait()
    own_f[...] = proj[...].astype(F32)
    for h in range(2):
        for q in range(4):
            for p in range(2):
                for c in range(2):
                    rows = own_f[pl.ds(p * RAW + 36 * q + 18 * h + c, 9, stride=2), :]
                    own_r[pl.ds(h * BLOCK + 36 * q + 2 * c + p, 9, stride=4), :] = rows
    for h in range(2):
        own_b[h, 0:BLOCK, :] = own_r[h * BLOCK:(h + 1) * BLOCK, :].astype(BF16)

    pl.semaphore_wait(barrier, 14 + jnp.where(z // 4 == core, 6, 8) + jnp.where(edge, 2, 0))

    sent = []
    meta_copy = remote(meta.at[core], meta.at[core], pair)
    block_copy = remote(own_b.at[mate], lib_in.at[me], pair)
    img_copy = remote(img_hbm, img.at[core], pair)
    far_sends, far_slots, first_slots, second_slots = [], [], [], []
    for first, count, length in LIB_CHUNKS:
        rows = pl.ds(first * 4, length)
        pick = [next(recv_slots), next(recv_slots)]
        far_slots.append(pick)
        for py in (beyond[1], beyond[0]):
            for h in range(2):
                far_sends.append(
                    remote(own_b.at[h, rows], lib_in.at[me, rows], device(x, py, z, h), pick[0] + core)
                )

    @pl.when(edge)
    def _():
        for copy in far_sends[:8]:
            copy.start()

    def to_peers(chunk):
        first, count, length = LIB_CHUNKS[chunk]
        rows = pl.ds(first * 4, length)
        for d in (2, 1, 3):
            pick = [next(recv_slots), next(recv_slots)]
            first_slots.append(pick)
            for h in range(2):
                copy = remote(
                    own_b.at[h, rows], lib_in.at[me, rows], device((x + d) % 4, y, z, h), pick[0] + core
                )
                copy.start()
                sent.append(copy)

    to_peers(0)
    to_peers(1)

    copies[5].wait()
    lane8 = lax.broadcasted_iota(jnp.int32, (8, 128), 1)
    tile = jnp.zeros((8, 128), F32)
    for p in range(2):
        re = own_f[pl.ds(p * RAW, TILES, stride=2), :]
        im = own_f[pl.ds(p * RAW + 1, TILES, stride=2), :]
        own_p[p] = re * re + im * im
    sums = [jnp.zeros((8, 128), F32)] * 8
    for t in range(TILES):
        c = ctf[:, t * 128:(t + 1) * 128]
        c = c * c
        for p in range(2):
            k = 2 * (t % 4) + p
            sums[k] = sums[k] + c * jnp.broadcast_to(own_p[p, pl.ds(t, 1), :], (8, 128))
    for p in range(2):
        power = jnp.sum((sums[p] + sums[2 + p]) + (sums[4 + p] + sums[6 + p]), axis=1, keepdims=True)
        hi = power.astype(BF16).astype(F32)
        mid = (power - hi).astype(BF16).astype(F32)
        column = core * 16 + p * 8 + x * 2 + yh
        for k, part in enumerate((hi, mid, power - hi - mid)):
            tile = tile + jnp.where(lane8 == column + 32 * k, part, 0.0)
    tile = jnp.concatenate([tile, jnp.zeros((8, 128), F32)], axis=0).astype(BF16)
    own_b[0, pl.ds(BLOCK, 16), :] = tile
    own_b[1, pl.ds(BLOCK, 16), :] = tile

    @pl.when(edge)
    def _():
        for copy in far_sends[8:]:
            copy.start()

    to_peers(2)
    lib_in[me] = own_b[core]
    for copy in (block_copy, img_copy):
        copy.start()
        sent.append(copy)

    for copy in copies[1:4]:
        copy.wait()

    lane24 = lax.broadcasted_iota(jnp.int32, (CAP, 128), 1)
    alive = lax.broadcasted_iota(jnp.int32, (CAP, 1), 0) < counts_v[...]
    meta[core] = jnp.where(
        lane24 == 0, column_of(classes_v[...].astype(F32), CAP),
        jnp.where(lane24 == 1, column_of(precision_v[...], CAP), jnp.where(alive, 1.0, 0.0)),
    )
    def three_parts(v):
        hi = v.astype(BF16).astype(F32)
        mid = (v - hi).astype(BF16).astype(F32)
        return jnp.concatenate([hi, mid, v - hi - mid], axis=0).astype(BF16)

    def prepare(who):
        klass = meta[who][:, 0:1]
        kinds = lax.broadcasted_iota(jnp.int32, (CAP, CLASSES), 1).astype(F32)
        onehot = (klass == kinds).astype(F32)
        pick = jnp.concatenate([onehot, onehot, onehot], axis=1).astype(BF16)
        for q in range(4):
            c = ctf[:, pl.ds(pl.multiple_of((18 * q + base) * 128, 128), 1152)]
            parts = three_parts(c)
            crow[:, q * 1152:(q + 1) * 1152] = jnp.dot(pick, parts, preferred_element_type=F32)

        def widen(n, carry):
            rows = pl.ds(pl.multiple_of(n * RAW, 16), RAW)
            raw[rows, :] = img[who, rows, :].astype(F32)
            return carry

        lax.fori_loop(0, CAP, widen, 0)

    zeros8 = jnp.zeros((8, 128), F32)

    def shift_tiles(who, i, carry):
        q, v = i // 3, i % 3
        for u in range(3):
            t = 18 * q + base + 3 * v + u
            tt = 3 * i + u
            cols = pl.ds(pl.multiple_of(tt * 128, 128), 128)
            real, imag = [], []
            for g in range(3):
                c = crow[8 * g:8 * g + 8, cols]
                real.append(raw[pl.ds(g * 8 * RAW + 2 * t, 8, stride=RAW), :] * c)
                imag.append(raw[pl.ds(g * 8 * RAW + 2 * t + 1, 8, stride=RAW), :] * c)
            pairs = []
            for k in range(SHIFTS * 3 + 1):
                s, g = k // 3, k % 3
                if s < SHIFTS:
                    if g == 0:
                        cs = jnp.broadcast_to(phases[0, pl.ds(s, 1), cols], (8, 128))
                        sn = jnp.broadcast_to(phases[1, pl.ds(s, 1), cols], (8, 128))
                    ac, bs = real[g] * cs, imag[g] * sn
                    bc, as_ = imag[g] * cs, real[g] * sn
                    pairs.append((ac + bs, bc - as_, ac - bs, bc + as_))
                else:
                    pairs.append((zeros8,) * 4)
                if k % 2:
                    for j, (dst, half) in enumerate(((shifted, 0), (shifted, 1), (back, 0), (back, 1))):
                        wide = pl.ds(pl.multiple_of(tt * 256 + half * 128, 128), 128)
                        both = jnp.concatenate([pairs[0][j], pairs[1][j]], axis=0).astype(BF16)
                        dst[pl.ds(pl.multiple_of(who * ROWS + 8 * (k - 1), 16), 16), wide] = both
                    pairs = []
        return carry

    meta_copy.start()
    sent.append(meta_copy)


    copies[4].wait()
    step = shifts_v[...].astype(F32)
    step_x = jnp.broadcast_to(column_of(step[0:1, :], 16), (16, 128))
    step_y = jnp.broadcast_to(column_of(step[1:2, :], 16), (16, 128))
    fine = []
    lanes = lax.broadcasted_iota(jnp.int32, (16, 128), 1)

    def turned_by(steps):
        steps = steps - 192.0 * jnp.floor(steps * (1.0 / 192.0) + 0.5)
        h = steps * (0.5 * STEP)
        h2 = h * h
        sn, cs = jnp.zeros_like(h), jnp.zeros_like(h)
        for k in range(7, -1, -1):
            sn = sn * h2 + (-1.0) ** k / math.factorial(2 * k + 1)
            cs = cs * h2 + (-1.0) ** k / math.factorial(2 * k)
        sn = sn * h
        return 1.0 - 2.0 * (sn * sn), 2.0 * (sn * cs)

    for u in range(3):
        j = lanes + u * 128
        dy = (j >= 96).astype(jnp.int32) + (j >= 192).astype(jnp.int32) + (j >= 288).astype(jnp.int32)
        kx = j - 96 * dy
        fine.append(turned_by(step_x * kx.astype(F32) + step_y * dy.astype(F32)))
    rows_on = jnp.where(lanes == 0, 12 * core - FREQ // 2, jnp.where(lanes == 1, 4, 16)).astype(F32)
    coarse = turned_by(step_y * rows_on)
    start_c, turn_c, leap_c = [jnp.broadcast_to(coarse[0][:, k:k + 1], (16, 128)) for k in range(3)]
    start_s, turn_s, leap_s = [jnp.broadcast_to(coarse[1][:, k:k + 1], (16, 128)) for k in range(3)]

    def table(i, carry):
        base_c, base_s = carry
        for u in range(3):
            fc, fs = fine[u]
            cols = pl.ds(pl.multiple_of((3 * i + u) * 128, 128), 128)
            phases[0, :, cols] = fc * base_c - fs * base_s
            phases[1, :, cols] = fs * base_c + fc * base_s
        last = i % 3 == 2
        tc, ts = jnp.where(last, leap_c, turn_c), jnp.where(last, leap_s, turn_s)
        return base_c * tc - base_s * ts, base_s * tc + base_c * ts

    lax.fori_loop(0, 12, table, (start_c, start_s))

    copies[6].wait()
    prepare(core)

    other = (x * 2 + 1 - yh) * 2

    def hand_on(chunk):
        first, count, length = LIB_CHUNKS[chunk]
        rows = pl.ds(first * 4, length)
        for k in range(2):
            arrival(lib_in.at[other + k, rows], far_slots[chunk][k]).wait_recv()
        slots = []
        view = lib_in.at[pl.ds(other, 2), rows]
        for d in (2, 1, 3):
            copy = remote(view, view, device((x + d) % 4, y, z, core))
            copy.start()
            sent.append(copy)
            slots.append(copy)
        second_slots.append(slots)

    lax.fori_loop(0, 12, functools.partial(shift_tiles, core), 0, unroll=2)

    hand_on(0)

    arrival(meta.at[mate], 0).wait_recv()
    arrival(img.at[mate], 2).wait_recv()
    prepare(mate)
    lax.fori_loop(0, 2, functools.partial(shift_tiles, mate), 0, unroll=2)
    hand_on(1)
    lax.fori_loop(2, 6, functools.partial(shift_tiles, mate), 0, unroll=2)
    hand_on(2)
    lax.fori_loop(6, 12, functools.partial(shift_tiles, mate), 0, unroll=2)

    total = jnp.zeros((2 * ROWS, POSES), F32)
    arrival(lib_in.at[0], 1).wait_recv()
    for chunk, (first, count, length) in enumerate(LIB_CHUNKS):
        rows = pl.ds(first * 4, length)
        for pick in first_slots[3 * chunk:3 * chunk + 3]:
            for slot in pick:
                arrival(lib_in.at[0, rows], slot).wait_recv()
        for copy in second_slots[chunk]:
            copy.wait_recv()

        def widen_lib(k, carry):
            tiles = pl.ds(first * 4, count * 4)
            lib_f[pl.ds(pl.multiple_of(k * BLOCK + first * 4, 16), count * 4), :] = lib_in[k, tiles, :].astype(F32)
            return carry

        lax.fori_loop(0, 16, widen_lib, 0)

        def gather_tiles(i, carry):
            for u in range(4):
                tt = first + i * 4 + u
                halves = []
                for k in range(2):
                    parts = [
                        lib_f[pl.ds(c * BLOCK + tt * 4 + k * 2 + p, 8, stride=2 * BLOCK), :]
                        for c in range(2) for p in range(2)
                    ]
                    halves.append(jnp.concatenate(parts, axis=0))
                cols = pl.ds(pl.multiple_of(tt * 256, 256), 256)
                lib_b[:, cols] = jnp.concatenate(halves, axis=1).astype(BF16)
            return carry

        lax.fori_loop(0, count // 4, gather_tiles, 0)
        cols = slice(first * 256, (first + count) * 256)
        total = total + lax.dot_general(
            shifted[:, cols], lib_b[:, cols], (((1,), (1,)), ((), ())), preferred_element_type=F32
        )
    powers = jnp.zeros((8, 128), F32)
    for k in range(16):
        powers = powers + lib_in[k, pl.ds(BLOCK, 16), :].astype(F32)[0:8, :]
    powers = powers[:, 0:32] + powers[:, 32:64] + powers[:, 64:96]
    klass = [meta[c][:, 0:1] for c in range(2)]
    parts, bias = [], []
    for c in range(2):
        class_power = jnp.zeros((CAP, POSES), F32)
        for k in range(CLASSES):
            class_power = class_power + jnp.where(klass[c] == float(k), powers[k:k + 1, :], 0.0)
        bias.append(0.5 * class_power)
        parts.append([total[c * ROWS + s * CAP:c * ROWS + (s + 1) * CAP, :] for s in range(SHIFTS)])
        for s in range(SHIFTS):
            mine[c, s * CAP:(s + 1) * CAP, 0:POSES] = parts[c][s]
    score_copy = remote(mine, theirs, pair)
    score_copy.start()
    sent.append(score_copy)
    score_copy.wait_recv()
    log_norm, weights = [], []
    for c in range(2):
        prec, live = meta[c][:, 1:2], meta[c][:, 2:3] > 0.5
        scores = [prec * (parts[c][s] + theirs[c, s * CAP:(s + 1) * CAP, 0:POSES] - bias[c]) for s in range(SHIFTS)]
        top = scores[0]
        for s in range(1, SHIFTS):
            top = jnp.maximum(top, scores[s])
        top = jnp.max(top, axis=1, keepdims=True)
        mass = jnp.exp(scores[0] - top)
        for s in range(1, SHIFTS):
            mass = mass + jnp.exp(scores[s] - top)
        norm = top + jnp.log(jnp.sum(mass, axis=1, keepdims=True))
        log_norm.append(jnp.where(live, norm, 0.0))
        weights += [jnp.where(live, jnp.exp(v - norm), 0.0) for v in scores] + [jnp.zeros((8, POSES), F32)]
    weight = jnp.concatenate(weights, axis=0).astype(BF16)
    unit = lax.broadcasted_iota(jnp.int32, (POSES, POSES), 0) == lax.broadcasted_iota(jnp.int32, (POSES, POSES), 1)
    weight_t = lax.dot_general(
        unit.astype(F32).astype(BF16), weight, (((1,), (1,)), ((), ())), preferred_element_type=F32
    ).astype(BF16)

    def sum_tiles(first, count):
        def sum_quarter(q, carry):
            cols = pl.ds(pl.multiple_of((q * 9 + first) * 256, 256), count * 256)
            part = jnp.dot(weight_t, back[:, cols], preferred_element_type=F32)
            for c in range(2):
                for p in range(2):
                    r = c * 16 + p * 8
                    for k in range(2 * count):
                        row = 256 * first + (q * count + k // 2) * 8 + c * 4 + (k % 2) * 2 + p
                        acc[pl.ds(row, 8, stride=32 * count), :] = part[r:r + 8, k * 128:(k + 1) * 128]
            return carry

        lax.fori_loop(0, 4, sum_quarter, 0)

    sum_tiles(0, LEAD)
    lead_rows = 8 * LEAD
    for g in range(8):
        for px in range(4):
            rows = pl.ds(px * lead_rows, lead_rows)
            lead_out[g, rows, :] = acc[(px * 8 + g) * lead_rows:(px * 8 + g + 1) * lead_rows, :].astype(BF16)
    lead_sends = []
    for d in (4, 3, 5, 2, 6, 1, 7):
        py = (y + d) % 8
        copy = remote(lead_out.at[py], lead_in.at[d - 1], device(x, py, z, core))
        copy.start()
        lead_sends.append(copy)
    sent += lead_sends

    x_sends = []
    for first, count in CHUNKS:
        rows = pl.ds(64 * first, 64 * count)
        sum_tiles(first, count)
        chunk_sends = []
        for d in (2, 1, 3):
            at = pl.multiple_of(256 * first + (x + d) % 4 * 64 * count, 64)
            x_out[d - 1, rows, :] = acc[pl.ds(at, 64 * count), :].astype(BF16)
            copy = remote(x_out.at[d - 1, rows], x_in.at[d - 1, rows], device((x + d) % 4, y, z, core))
            copy.start()
            chunk_sends.append(copy)
        x_sends.append(chunk_sends)
        sent += chunk_sends
    shown = jnp.where(core == 0, log_norm[0], log_norm[1])
    r24 = lax.broadcasted_iota(jnp.int32, (CAP, 128), 0)
    norm_ref[...] = jnp.sum(jnp.where(r24 == lane24, shown, 0.0), axis=0, keepdims=True)

    y_sends = []
    for (first, count), chunk_sends in zip(CHUNKS, x_sends):
        rows = pl.ds(64 * first, 64 * count)
        size = 8 * count
        for copy in chunk_sends:
            copy.wait_recv()
        part = acc[pl.ds(pl.multiple_of(256 * first + x * 64 * count, 64), 64 * count), :]
        for d in range(3):
            part = part + x_in[d, rows, :].astype(F32)
        room = pl.ds(8 * first, 16)
        for g in range(8):
            piece = part[g * size:(g + 1) * size, :]
            y_own[g, pl.ds(8 * first, size), :] = piece
            if size < 16:
                piece = jnp.concatenate([piece, zeros8], axis=0)
            y_out[g, room, :] = piece.astype(BF16)
        chunk_sends = []
        for d in (4, 3, 5, 2, 6, 1, 7):
            py = (y + d) % 8
            copy = remote(y_out.at[py, room], y_in.at[d - 1, room], device(x, py, z, core))
            copy.start()
            chunk_sends.append(copy)
        y_sends.append(chunk_sends)
        sent += chunk_sends
    for copy in lead_sends:
        copy.wait_recv()
    part = jnp.concatenate(
        [acc[pl.ds(pl.multiple_of((px * 8 + y) * lead_rows, 16), lead_rows), :] for px in range(4)], axis=0
    )
    for d in range(7):
        part = part + lead_in[d].astype(F32)
    for px in range(4):
        piece = part[px * lead_rows:(px + 1) * lead_rows, :]
        last_own[px] = piece
        last_out[px] = piece.astype(BF16)
    last_sends = []
    for d in (2, 1, 3):
        px = (x + d) % 4
        copy = remote(last_out.at[px], last_in.at[d - 1], device(px, y, z, core))
        copy.start()
        last_sends.append(copy)
    sent += last_sends

    for (first, count), chunk_sends in zip(CHUNKS, y_sends):
        size = 8 * count
        for copy in chunk_sends:
            copy.wait_recv()
        part = y_own[y, pl.ds(8 * first, size), :]
        for d in range(7):
            part = part + y_in[d, pl.ds(8 * first, 16), :].astype(F32)[0:size, :]
        z_own[pl.ds(8 * first, size), :] = part

    for copy in last_sends:
        copy.wait_recv()
    part = last_own[x]
    for d in range(3):
        part = part + last_in[d].astype(F32)
    z_own[0:lead_rows, :] = part

    zeros4 = jnp.zeros((4, 128), F32)
    for k in range(4):
        for c in range(2):
            for i in range(3):
                first = (2 * k + i) * 8 + c * 4
                z_f[2 * k + c, 4 * i:4 * i + 4, :] = z_own[first:first + 4, :]
            z_f[2 * k + c, 12:16, :] = zeros4
            z_out[2 * k + c] = z_f[2 * k + c].astype(BF16)
    z_first = next(recv_slots)
    for _ in range(7):
        next(recv_slots)
    own_place = z // 4 == core
    z_sends = []
    for d in (2, 1, 3, 0):
        k = (z + d) % 4
        for c in (mate, core):
            z_sends.append(remote(
                z_out.at[2 * k + c], z_in.at[z], device(x, y, 4 * core + k, c), z_first + z
            ))
    for copy in z_sends[:-1]:
        copy.start()
    sent += z_sends[:-1]

    @pl.when(own_place)
    def _():
        z_in[z] = z_out[2 * (z % 4) + core]

    @pl.when(jnp.logical_not(own_place))
    def _():
        z_sends[-1].start()

    for k in range(8):
        @pl.when(jnp.logical_not(jnp.logical_and(own_place, z == k)))
        def _():
            arrival(z_in.at[k], z_first + k).wait_recv()

    part = z_in[0].astype(F32)
    for k in range(1, 8):
        part = part + z_in[k].astype(F32)
    skip = (z % 4) * 32
    turned = pltpu.roll(part, (128 - skip) % 128, 1)
    keep = lax.broadcasted_iota(jnp.int32, (4, 128), 1) < 128 - skip
    for t in range(3):
        piece = turned[4 * t:4 * t + 4, :]
        if t < 2:
            piece = jnp.where(keep, piece, turned[4 * t + 4:4 * t + 8, :])
        for p in range(2):
            for c in range(2):
                accum_ref[p, c:c + 1, t * 128:t * 128 + 128] = piece[c * 2 + p:c * 2 + p + 1, :]

    for copy in sent:
        copy.wait_send()

    @pl.when(edge)
    def _():
        for copy in far_sends:
            copy.wait_send()

    @pl.when(jnp.logical_not(own_place))
    def _():
        z_sends[-1].wait_send()


def body(images, classes, precision, counts, shifts, ctf_table, projections):
    raw_img = images.reshape(CAP, 2, TILES, 128).transpose(0, 2, 1, 3).reshape(CAP * RAW, 128)
    raw_proj = projections.reshape(2, 2, TILES, 128).transpose(0, 2, 1, 3).reshape(2 * RAW, 128)
    vmem = pl.BlockSpec(memory_space=pltpu.VMEM)
    anywhere = pl.BlockSpec(memory_space=pl.ANY)
    accum, norm = pl.pallas_call(
        kernel,
        out_shape=(
            jax.ShapeDtypeStruct((2, 2, 384), F32),
            jax.ShapeDtypeStruct((1, 128), F32),
        ),
        in_specs=[anywhere] * 7,
        out_specs=(vmem, vmem),
        scratch_shapes=[
            pltpu.VMEM((1, CAP), jnp.int32),
            pltpu.VMEM((1, CAP), F32),
            pltpu.VMEM((1, 1), jnp.int32),
            pltpu.VMEM((2, SHIFTS), jnp.int32),
            pltpu.VMEM((2 * RAW, 128), BF16),
            pltpu.VMEM((2, CAP * RAW, 128), BF16),
            pltpu.VMEM((CLASSES, HALF), F32),
            pltpu.VMEM((CAP * RAW, 128), F32),
            pltpu.VMEM((CAP, HALF // 2), F32),
            pltpu.VMEM((2, 16, HALF // 2), F32),
            pltpu.VMEM((2 * ROWS, HALF), BF16),
            pltpu.VMEM((2 * ROWS, HALF), BF16),
            pltpu.VMEM((2, CAP, 128), F32),
            pltpu.VMEM((2 * RAW, 128), F32),
            pltpu.VMEM((2 * BLOCK, 128), F32),
            pltpu.VMEM((2, TILES, 128), F32),
            pltpu.VMEM((2, FULL, 128), BF16),
            pltpu.VMEM((16, FULL, 128), BF16),
            pltpu.VMEM((16 * BLOCK, 128), F32),
            pltpu.VMEM((POSES, HALF), BF16),
            pltpu.VMEM((2, ROWS, 128), F32),
            pltpu.VMEM((2, ROWS, 128), F32),
            pltpu.VMEM((32 * 72, 128), F32),
            pltpu.VMEM((3, 576, 128), BF16),
            pltpu.VMEM((3, 576, 128), BF16),
            pltpu.VMEM((8, 72, 128), F32),
            pltpu.VMEM((8, 80, 128), BF16),
            pltpu.VMEM((7, 80, 128), BF16),
            pltpu.VMEM((8, 32 * LEAD, 128), BF16),
            pltpu.VMEM((7, 32 * LEAD, 128), BF16),
            pltpu.VMEM((4, 8 * LEAD, 128), F32),
            pltpu.VMEM((4, 8 * LEAD, 128), BF16),
            pltpu.VMEM((3, 8 * LEAD, 128), BF16),
            pltpu.VMEM((72, 128), F32),
            pltpu.VMEM((8, 16, 128), F32),
            pltpu.VMEM((8, 16, 128), BF16),
            pltpu.VMEM((8, 16, 128), BF16),
            pltpu.SemaphoreType.DMA((7,)),
            pltpu.SemaphoreType.DMA((128,)),
            pltpu.SemaphoreType.DMA((128,)),
        ],
        compiler_params=pltpu.CompilerParams(
            collective_id=0, has_side_effects=True, vmem_limit_bytes=56 * 1024 * 1024
        ),
        name="expectation",
    )(
        classes.reshape(1, CAP), precision.reshape(1, CAP), counts.reshape(1, 1), shifts.T,
        raw_img, ctf_table, raw_proj,
    )
    return accum[:, :, :HALF // 32], norm.reshape(128)[:CAP]


def solution(mesh):
    placed = (
        P(("lib", "dom"), None, None),
        P(("lib", "dom")),
        P(("lib", "dom")),
        P(("lib", "dom")),
        P(),
        P(),
        P("lib", None, None),
    )
    return jax.shard_map(
        body,
        mesh=mesh,
        in_specs=placed,
        out_specs=(P("lib", None, "dom"), P(("lib", "dom"))),
        check_vma=False,
    )
```
